512 devices in a mesh: row: 64 (over x, z), col: 8 (over y, core).
Axes of the slice: x: 4, y: 4, z: 16, core: 2. Of those that a mesh axis runs over, the one named last changes fastest.
Arguments:
- coarse_kernel: bfloat16 [32768, 2048], P('row', 'col'), may hold values from -6 to 6
- row_cond: bfloat16 [1024, 8, 16], P(('row', 'col')), may hold values from -1.796875 to 1.796875
- row_val: bfloat16 [1024, 4, 8], P(('row', 'col')), may hold values from -1.796875 to 1.796875
- col_cond: bfloat16 [64, 8, 16], P('col'), may hold values from -1.796875 to 1.796875
- col_val: bfloat16 [64, 4, 8], P('col'), may hold values from -1.796875 to 1.796875
- near_row: int32 [1024], replicated, may hold values from 0 to 255, as said below
- owner_map: int32 [256], replicated, may hold values from 0 to 255, as said below
- near_col: int32 [64], P('col'), may hold values from 0 to 1
Outputs:
- fine_kernel: bfloat16 [32768, 2048], P('row', 'col')
The draws below stay inside these ranges and needn't reach their ends.
Inputs may be any that keep to these rules, and one draw needn't show every extreme that they name: Fine row r's coarse point is stored on row index owner_map[near_row[r]] // 4. Among the 16 fine rows of one row index at most 2 have their coarse point on one row index, and in every such block some row index serves exactly 2 of them. `owner_map`: A permutation: every slot holds one coarse row k-point.
All inputs are finite; a program needn't handle non-finite values.
Results may differ from the reference program's by a relative error of at most 0.0057.
Values may be sent and summed in bfloat16 or wider, within the bound.
A program may use at most 128 MiB of HBM per device.

```python
import jax
import jax.numpy as jnp
from jax import lax

CF = 8
VF = 4
CC = 16
VC = 8
TC = 128
FR = 16
FC = 8
CCD = 2
CAP = 2
CRD = 4
NCR = 256
NFR = 1024
NFC = 64
NCC = 16


def storage_order(key):
    return jax.random.permutation(key, NCR).astype(jnp.int32)


def draw_owner_map(key, part):
    return storage_order(key)


def draw_near_row(key, part):
    ordering = storage_order(key)
    key = jax.random.fold_in(key, 7)
    inverse = jnp.argsort(ordering).astype(jnp.int32)
    blocks = NFR // FR
    owners_count = NCR // CRD
    hot_key, pick_key, point_key = jax.random.split(key, 3)
    hottest = jax.random.randint(hot_key, (blocks,), 0, owners_count).astype(jnp.int32)
    repeated = jnp.arange((owners_count - 1) * CAP, dtype=jnp.int32) // CAP

    def one_block(block_key, hot_owner):
        draw_key, shuffle_key = jax.random.split(block_key)
        picked = jax.random.permutation(draw_key, repeated)[:FR - CAP]
        others = (hot_owner + 1 + picked) % owners_count
        owners = jnp.concatenate([jnp.full((CAP,), hot_owner, jnp.int32), others.astype(jnp.int32)])
        return jax.random.permutation(shuffle_key, owners)
    owners = jax.vmap(one_block)(jax.random.split(pick_key, blocks), hottest).reshape(NFR)
    points = jax.random.randint(point_key, (NFR,), 0, CRD).astype(jnp.int32)
    return jnp.take(inverse, owners * CRD + points).astype(jnp.int32)


def touch_ends(result, stream_key, least, high):
    extent = result.shape
    spot = [jax.random.randint(jax.random.fold_in(stream_key, axis), (), 0, extent[axis]) for axis in range(len(extent))]
    result = result.at[tuple(spot)].set(least)
    longest = extent.index(max(extent))
    spot[longest] = (spot[longest] + 1) % extent[longest]
    return result.at[tuple(spot)].set(high)


def block_scale(rng, dims, cuts, least, largest):
    level = 1.0
    for axis_at, parts in cuts:
        draws = jax.random.uniform(jax.random.fold_in(jax.random.fold_in(rng, 6), axis_at), (parts,), jnp.float32, least / len(cuts), largest / len(cuts))
        level = level * jnp.repeat(jnp.exp(draws), dims[axis_at] // parts).reshape((-1,) + (1,) * (len(dims) - 1 - axis_at))
    return level


def bell_draw(key, dims, scale, limit, pieces=(), kind=jnp.bfloat16):
    factor_of = block_scale(key, dims, pieces, -0.22, 0.18) if pieces else 1.0
    drawn = jax.random.normal(key, dims, jnp.float32) * scale * factor_of
    return jnp.minimum(jnp.maximum(drawn, -limit), limit).astype(kind)


def setup_inputs(seed: int = 0) -> dict:
    arg_keys = jax.random.split(jax.random.key(seed), 9)
    coarse_kernel = bell_draw(arg_keys[0], (NCR * TC, NCC * TC), 1.0, 6.0, ((0, 64), (1, 8)))
    row_cond = bell_draw(arg_keys[1], (NFR, CF, CC), 0.3, 1.796875, ((0, 512),))
    row_val = bell_draw(arg_keys[2], (NFR, VF, VC), 0.3, 1.796875, ((0, 512),))
    col_cond = bell_draw(arg_keys[3], (NFC, CF, CC), 0.3, 1.796875, ((0, 8),))
    col_val = bell_draw(arg_keys[4], (NFC, VF, VC), 0.3, 1.796875, ((0, 8),))
    near_row = draw_near_row(jax.random.fold_in(arg_keys[8], 71), 0)
    owner_map = draw_owner_map(jax.random.fold_in(arg_keys[8], 71), 0)
    near_col = touch_ends(jax.random.randint(arg_keys[7], (NFC,), 0, CCD), jax.random.fold_in(arg_keys[7], 1), 0, CCD - 1).astype(jnp.int32)
    return dict(coarse_kernel=coarse_kernel, row_cond=row_cond, row_val=row_val, col_cond=col_cond, col_val=col_val, near_row=near_row, owner_map=owner_map, near_col=near_col)


def expand_pairs(conduction, valence):
    entries = conduction.shape[0]
    product = conduction.astype(jnp.float32)[:, :, None, :, None] * valence.astype(jnp.float32)[:, None, :, None, :]
    return product.reshape(entries, CF * VF, CC * VC).astype(jnp.bfloat16)


def reference(coarse_kernel, row_cond, row_val, col_cond, col_val, near_row, owner_map, near_col):
    trans_fine = CF * VF
    trans_coarse = CC * VC
    col_blocks = NFC // FC
    width = FC * trans_fine
    row_pairs = expand_pairs(row_cond, row_val)
    col_pairs = expand_pairs(col_cond, col_val).astype(jnp.float32)
    placed = (near_col.reshape(col_blocks, FC)[:, :, None] == jnp.arange(CCD, dtype=jnp.int32)[None, None, :]).astype(jnp.float32)
    pairs_blocked = col_pairs.reshape(col_blocks, FC, trans_fine, trans_coarse)
    kernel_blocked = jnp.transpose(coarse_kernel.reshape(NCR * trans_coarse, col_blocks, CCD * trans_coarse), (1, 0, 2))

    def column_block(operands):
        placed_block, pairs_block, kernel_block = operands
        spread = jnp.einsum("fc,ftb->cbft", placed_block, pairs_block).reshape(CCD * trans_coarse, width)
        return jnp.dot(kernel_block.astype(jnp.float32), spread, precision=lax.Precision.HIGHEST, preferred_element_type=jnp.float32)

    projected = lax.map(column_block, (placed, pairs_blocked, kernel_blocked))
    projected = projected.reshape(col_blocks, NCR, trans_coarse, width)
    row_slot = jnp.take(owner_map, near_row).astype(jnp.int32)
    row_groups = NFR // FR

    def row_block(operands):
        slots_block, pairs_block = operands
        selected = jnp.take(projected, slots_block, axis=1)
        rows_out = jnp.einsum("rta,jraw->rtjw", pairs_block.astype(jnp.float32), selected, precision=lax.Precision.HIGHEST)
        return rows_out.reshape(FR * trans_fine, col_blocks * width).astype(jnp.bfloat16)

    panel = lax.map(row_block, (row_slot.reshape(row_groups, FR), row_pairs.reshape(row_groups, FR, trans_fine, trans_coarse)))
    return panel.reshape(NFR * trans_fine, NFC * trans_fine)
```

```python
import functools

import jax
import jax.numpy as jnp
from jax import lax
from jax.experimental import pallas as pl
from jax.experimental.pallas import tpu as pltpu
from jax.sharding import PartitionSpec as P

MESH = pl.DeviceIdType.MESH
F32 = jnp.float32
BF16 = jnp.bfloat16
Z_SIZE = 16


def one_hot(shape, test):
    rows = lax.broadcasted_iota(jnp.int32, shape, 0)
    lanes = lax.broadcasted_iota(jnp.int32, shape, 1)
    return jnp.where(test(rows, lanes), 1.0, 0.0).astype(BF16)


def mm(a, b):
    return jnp.dot(a, b, preferred_element_type=F32)


def kernel(
    nx, nz, nc, cf, vf, cc, vc,
    coarse, row_cond, row_val, col_cond, col_val, near_row, owner_map, near_col,
    out,
    kbuf, work, fbuf, pbuf, smat, ybuf, ysend,
    own_s, enc_s, sel_s,
    ring_recv, ring_send, local_sem, fac_recv, fac_send, facx_recv, facx_send, x_recv, x_send,
):
    me = lax.axis_index("row")
    my_col = lax.axis_index("col")
    my_x, my_z = me // nz, me % nz
    half = nz // 2
    tc, tf = cc * vc, cf * vf
    points = coarse.shape[0] // tc
    shift = points.bit_length() - 1
    assert points == 1 << shift
    fine_rows = out.shape[0] // tf
    width = out.shape[1]
    my_rows = row_cond.shape[0]
    fac_rows = my_rows * cf

    z_up = (my_x * nz + (my_z + 1) % nz, my_col)
    z_down = (my_x * nz + (my_z + nz - 1) % nz, my_col)
    x_peer = [(((my_x + d) % nx) * nz + my_z, my_col) for d in range(nx)]
    col_peer = [(me, (my_col + d) % nc) for d in range(nc)]

    barrier = pltpu.get_barrier_semaphore()
    peers = [z_up, z_down] + x_peer[1:] + col_peer[1:]
    for peer in peers:
        pl.semaphore_signal(barrier, inc=1, device_id=peer, device_id_type=MESH)

    local = pltpu.make_async_copy(coarse, kbuf.at[my_z], local_sem)
    local.start()
    cond = row_cond[...].astype(F32).reshape(fac_rows, cc).astype(BF16)
    val = row_val[...].astype(F32)
    val = jnp.concatenate([val] * (cf // vf), axis=1).reshape(fac_rows, vc).astype(BF16)
    packed = mm(cond, one_hot((cc, 128), lambda k, l: l == k)) + mm(
        val, one_hot((vc, 128), lambda k, l: l == k + cc)
    )
    fbuf[my_x, pl.ds(my_col * fac_rows, fac_rows), :] = packed.astype(BF16)
    pl.semaphore_wait(barrier, len(peers))

    def ring_copy(way, hop, piece, src, first=False):
        rows = pl.ds(piece * tc, tc)
        source = coarse.at[rows, :] if first else kbuf.at[src, rows, :]
        return pltpu.make_async_remote_copy(
            src_ref=source,
            dst_ref=kbuf.at[src, rows, :],
            send_sem=ring_send,
            recv_sem=ring_recv.at[way, hop, piece],
            device_id=z_up if way == 0 else z_down,
            device_id_type=MESH,
        )

    def arrived(way, hop):
        return (my_z + nz - hop) % nz if way == 0 else (my_z + hop) % nz

    for piece in range(points):
        for way in (0, 1):
            ring_copy(way, 1, piece, my_z, first=True).start()

    mine = fbuf.at[my_x, pl.ds(my_col * fac_rows, fac_rows), :]
    for d in range(1, nc):
        pltpu.make_async_remote_copy(
            src_ref=mine, dst_ref=mine, send_sem=fac_send, recv_sem=fac_recv,
            device_id=col_peer[d], device_id_type=MESH,
        ).start()

    def slot_entry(k, carry):
        x, i = k // fine_rows, k % fine_rows
        slot = owner_map[near_row[(x * nz + my_z) * fine_rows + i]]
        own_s[k] = slot >> shift
        enc_s[k] = (i << shift) + (slot & (points - 1))
        return carry

    lax.fori_loop(0, nx * fine_rows, slot_entry, 0)

    others = fbuf.at[my_x, pl.ds(0, (nc - 1) * fac_rows), :]
    fac_all = pltpu.make_async_remote_copy(
        src_ref=others, dst_ref=others, send_sem=fac_send, recv_sem=fac_recv,
        device_id=col_peer[1], device_id_type=MESH,
    )
    fac_all.wait_recv()

    def facx_copy(source_x, d):
        return pltpu.make_async_remote_copy(
            src_ref=fbuf.at[source_x], dst_ref=fbuf.at[source_x], send_sem=facx_send.at[d],
            recv_sem=facx_recv.at[d], device_id=x_peer[d], device_id_type=MESH,
        )

    for d in range(1, nx):
        facx_copy(my_x, d).start()

    def spread_cond(k, l):
        return (k < cc) & (l // vc == k)

    def spread_val(k, l):
        return (k >= cc) & (k < cc + vc) & (l % vc == k - cc)

    def pairs(factors, entries):
        rows = entries * cf
        conds = mm(factors, one_hot((128, tc), spread_cond)).astype(BF16)
        vals = mm(factors, one_hot((128, tc), spread_val)).astype(BF16)
        left = mm(one_hot((entries * tf, rows), lambda t, k: t // vf == k), conds)
        right = mm(
            one_hot((entries * tf, rows), lambda t, k: (t // tf) * cf + t % vf == k), vals
        )
        return left * right

    fine_cols = col_cond.shape[0]
    ccond = col_cond[...].astype(F32).reshape(fine_cols * cf, cc).astype(BF16)
    cval = col_val[...].astype(F32)
    cval = jnp.concatenate([cval] * (cf // vf), axis=1).reshape(fine_cols * cf, vc).astype(BF16)
    cpacked = mm(ccond, one_hot((cc, 128), lambda k, l: l == k)) + mm(
        cval, one_hot((vc, 128), lambda k, l: l == k + cc)
    )
    right_pairs = pairs(cpacked.astype(BF16), fine_cols).T
    lane_point = jnp.zeros((1, width), jnp.int32)
    lane_f = lax.broadcasted_iota(jnp.int32, (1, width), 1) // tf
    for f in range(fine_cols):
        lane_point = jnp.where(lane_f == f, near_col[f], lane_point)
    for c in range(coarse.shape[1] // tc):
        smat[c * tc:(c + 1) * tc, :] = jnp.where(lane_point == c, right_pairs, 0.0).astype(BF16)

    for i in range(fine_rows):
        o = own_s[my_x * fine_rows + i]
        second = jnp.int32(0)
        for k in range(i):
            second = jnp.where(own_s[my_x * fine_rows + k] == o, 1, second)
        sel_s[i] = o * 2 + second

    def finish(z_src):
        o = my_x * nz + z_src
        work[...] = kbuf[z_src].reshape(work.shape)
        parts = []
        for d in range(nx):
            x = (my_x + d) % nx
            first, last = jnp.int32(0), jnp.int32(0)
            hits = []
            for i in range(fine_rows):
                hits.append((own_s[x * fine_rows + i] == o, enc_s[x * fine_rows + i]))
            for i in range(fine_rows):
                last = jnp.where(hits[i][0], hits[i][1], last)
                j = fine_rows - 1 - i
                first = jnp.where(hits[j][0], hits[j][1], first)
            for entry in (first, last):
                parts.append(mm(pbuf[x, entry >> shift], work[entry & (points - 1)]))
        partial = jnp.concatenate(parts, axis=0)
        high = partial.astype(BF16)
        low = (partial - high.astype(F32)).astype(BF16)
        done = (mm(high, smat[...]) + mm(low, smat[...])).astype(BF16)
        done = done.reshape(nx, 2, tf, width)
        ybuf[pl.ds(o * 2, 2)] = done[0]
        for d in range(1, nx):
            ysend[z_src, d - 1] = done[d]
            pltpu.make_async_remote_copy(
                src_ref=ysend.at[z_src, d - 1], dst_ref=ybuf.at[pl.ds(o * 2, 2)], send_sem=x_send,
                recv_sem=x_recv.at[d], device_id=x_peer[d], device_id_type=MESH,
            ).start()

    local.wait()
    for d in range(1, nx):
        facx_copy((my_x + nx - d) % nx, d).wait_recv()
    for x in range(nx):
        pbuf[x] = pairs(fbuf[x], fine_rows).astype(BF16).reshape(fine_rows, tf, tc)
    finish(my_z)

    def hop_step(hop, carry):
        for piece in range(points):
            for way in (0, 1):
                z_src = arrived(way, hop - 1)
                ring_copy(way, hop - 1, piece, z_src).wait_recv()
                ring_copy(way, hop, piece, z_src).start()
        for way in (0, 1):
            finish(arrived(way, hop - 1))
        return carry

    lax.fori_loop(2, half, hop_step, 0)
    for piece in range(points):
        for way in (0, 1):
            z_src = arrived(way, half - 1)
            ring_copy(way, half - 1, piece, z_src).wait_recv()
            if (piece < points // 2) == (way == 0):
                ring_copy(way, half, piece, z_src).start()
    for way in (0, 1):
        finish(arrived(way, half - 1))
    for piece in range(points):
        way = 0 if piece < points // 2 else 1
        ring_copy(way, half, piece, arrived(way, half)).wait_recv()
    finish(arrived(0, half))

    for d in range(1, nx):
        x = (my_x + nx - d) % nx
        block = ybuf.at[pl.ds(x * nz * 2, nz * 2)]
        pltpu.make_async_remote_copy(
            src_ref=block, dst_ref=block, send_sem=x_send, recv_sem=x_recv.at[d],
            device_id=x_peer[d], device_id_type=MESH,
        ).wait_recv()
    for i in range(fine_rows):
        out[i * tf:(i + 1) * tf, :] = ybuf[sel_s[i]]

    ring = kbuf.at[pl.ds(0, nz - 1)]
    pltpu.make_async_remote_copy(
        src_ref=ring, dst_ref=ring, send_sem=ring_send, recv_sem=ring_recv.at[0, 0, 0],
        device_id=z_up, device_id_type=MESH,
    ).wait_send()
    fac_all.wait_send()
    for d in range(1, nx):
        facx_copy(my_x, d).wait_send()
    pltpu.make_async_remote_copy(
        src_ref=ysend, dst_ref=ysend, send_sem=x_send, recv_sem=x_recv.at[0],
        device_id=x_peer[1], device_id_type=MESH,
    ).wait_send()


def shards(nx, nz, nc, coarse, row_cond, row_val, col_cond, col_val, near_row, owner_map, near_col):
    cf, cc = row_cond.shape[1:]
    vf, vc = row_val.shape[1:]
    tc, tf = cc * vc, cf * vf
    points = coarse.shape[0] // tc
    fine_rows = row_cond.shape[0] * nc
    width = col_cond.shape[0] * tf
    span = coarse.shape[1]
    vmem = pl.BlockSpec(memory_space=pltpu.VMEM)
    smem = pl.BlockSpec(memory_space=pltpu.SMEM)
    return pl.pallas_call(
        functools.partial(kernel, nx, nz, nc, cf, vf, cc, vc),
        out_shape=jax.ShapeDtypeStruct((fine_rows * tf, width), BF16),
        in_specs=[pl.BlockSpec(memory_space=pl.ANY), vmem, vmem, vmem, vmem, smem, smem, smem],
        out_specs=vmem,
        scratch_shapes=[
            pltpu.VMEM((nz, points * tc, span), BF16),
            pltpu.VMEM((points, tc, span), BF16),
            pltpu.VMEM((nx, fine_rows * cf, 128), BF16),
            pltpu.VMEM((nx, fine_rows, tf, tc), BF16),
            pltpu.VMEM((span, width), BF16),
            pltpu.VMEM((nx * nz * 2, tf, width), BF16),
            pltpu.VMEM((nz, nx - 1, 2, tf, width), BF16),
            pltpu.SMEM((nx * fine_rows,), jnp.int32),
            pltpu.SMEM((nx * fine_rows,), jnp.int32),
            pltpu.SMEM((fine_rows,), jnp.int32),
            pltpu.SemaphoreType.DMA((2, nz // 2 + 1, points)),
            pltpu.SemaphoreType.DMA,
            pltpu.SemaphoreType.DMA,
            pltpu.SemaphoreType.DMA,
            pltpu.SemaphoreType.DMA,
            pltpu.SemaphoreType.DMA((nx,)),
            pltpu.SemaphoreType.DMA((nx,)),
            pltpu.SemaphoreType.DMA((nx,)),
            pltpu.SemaphoreType.DMA,
        ],
        compiler_params=pltpu.CompilerParams(
            collective_id=0, has_side_effects=True, vmem_limit_bytes=40 * 1024 * 1024
        ),
    )(coarse, row_cond, row_val, col_cond, col_val, near_row, owner_map, near_col)


def solution(mesh, nz=Z_SIZE):
    nx, nc = mesh.shape["row"] // nz, mesh.shape["col"]
    return jax.shard_map(
        functools.partial(shards, nx, nz, nc),
        mesh=mesh,
        in_specs=(
            P("row", "col"),
            P(("row", "col"), None, None),
            P(("row", "col"), None, None),
            P("col", None, None),
            P("col", None, None),
            P(),
            P(),
            P("col"),
        ),
        out_specs=P("row", "col"),
        check_vma=False,
    )
```

```python
import functools

import jax
import jax.numpy as jnp
from jax import lax
from jax.experimental import pallas as pl
from jax.experimental.pallas import tpu as pltpu
from jax.sharding import PartitionSpec as P

MESH = pl.DeviceIdType.MESH
F32 = jnp.float32
BF16 = jnp.bfloat16
Z_SIZE = 16


def one_hot(shape, test):
    rows = lax.broadcasted_iota(jnp.int32, shape, 0)
    lanes = lax.broadcasted_iota(jnp.int32, shape, 1)
    return jnp.where(test(rows, lanes), 1.0, 0.0).astype(BF16)


def mm(a, b):
    return jnp.dot(a, b, preferred_element_type=F32)


def kernel(
    nx, nz, nc, cf, vf, cc, vc,
    coarse, row_cond_in, row_val_in, col_cond_in, col_val_in, near_row_in, owner_map_in, near_col_in,
    out,
    row_cond, row_val, col_cond, col_val, near_row, owner_map, near_col,
    kbuf, work, fbuf, pbuf, smat, ybuf, ysend,
    own_s, enc_s, sel_s,
    ring_recv, ring_send, fetch_sem, local_sem, fac_recv, fac_send, facx_recv, facx_send, x_recv, x_send,
):
    me = lax.axis_index("row")
    my_col = lax.axis_index("col")
    my_x, my_z = me // nz, me % nz
    half = nz // 2
    tc, tf = cc * vc, cf * vf
    points = coarse.shape[0] // tc
    shift = points.bit_length() - 1
    assert points == 1 << shift
    fine_rows = out.shape[0] // tf
    width = out.shape[1]
    my_rows = row_cond.shape[0]
    fac_rows = my_rows * cf

    z_up = (my_x * nz + (my_z + 1) % nz, my_col)
    z_down = (my_x * nz + (my_z + nz - 1) % nz, my_col)
    x_peer = [(((my_x + d) % nx) * nz + my_z, my_col) for d in range(nx)]
    col_peer = [(me, (my_col + d) % nc) for d in range(nc)]

    barrier = pltpu.get_barrier_semaphore()
    peers = [z_up, z_down] + x_peer[1:] + col_peer[1:]
    for peer in peers:
        pl.semaphore_signal(barrier, inc=1, device_id=peer, device_id_type=MESH)

    fetches = [
        pltpu.make_async_copy(source, target, fetch_sem.at[k])
        for k, (source, target) in enumerate((
            (row_cond_in, row_cond), (row_val_in, row_val), (near_row_in, near_row),
            (owner_map_in, owner_map), (near_col_in, near_col), (col_cond_in, col_cond),
            (col_val_in, col_val),
        ))
    ]
    for fetch in fetches:
        fetch.start()
    local = pltpu.make_async_copy(coarse, kbuf.at[my_z], local_sem)
    local.start()
    for fetch in fetches[:2]:
        fetch.wait()
    cond = row_cond[...].astype(F32).reshape(fac_rows, cc).astype(BF16)
    val = row_val[...].astype(F32)
    val = jnp.concatenate([val] * (cf // vf), axis=1).reshape(fac_rows, vc).astype(BF16)
    packed = mm(cond, one_hot((cc, 128), lambda k, l: l == k)) + mm(
        val, one_hot((vc, 128), lambda k, l: l == k + cc)
    )
    fbuf[my_x, pl.ds(my_col * fac_rows, fac_rows), :] = packed.astype(BF16)
    pl.semaphore_wait(barrier, len(peers))

    def ring_copy(way, hop, piece, src, first=False):
        rows = pl.ds(piece * tc, tc)
        source = coarse.at[rows, :] if first else kbuf.at[src, rows, :]
        return pltpu.make_async_remote_copy(
            src_ref=source,
            dst_ref=kbuf.at[src, rows, :],
            send_sem=ring_send,
            recv_sem=ring_recv.at[way, hop, piece],
            device_id=z_up if way == 0 else z_down,
            device_id_type=MESH,
        )

    def arrived(way, hop):
        return (my_z + nz - hop) % nz if way == 0 else (my_z + hop) % nz

    for piece in range(points):
        for way in (0, 1):
            ring_copy(way, 1, piece, my_z, first=True).start()

    mine = fbuf.at[my_x, pl.ds(my_col * fac_rows, fac_rows), :]
    for d in range(1, nc):
        pltpu.make_async_remote_copy(
            src_ref=mine, dst_ref=mine, send_sem=fac_send, recv_sem=fac_recv,
            device_id=col_peer[d], device_id_type=MESH,
        ).start()

    for fetch in fetches[2:]:
        fetch.wait()

    def slot_entry(k, carry):
        x, i = k // fine_rows, k % fine_rows
        slot = owner_map[near_row[(x * nz + my_z) * fine_rows + i]]
        own_s[k] = slot >> shift
        enc_s[k] = (i << shift) + (slot & (points - 1))
        return carry

    lax.fori_loop(0, nx * fine_rows, slot_entry, 0)

    others = fbuf.at[my_x, pl.ds(0, (nc - 1) * fac_rows), :]
    fac_all = pltpu.make_async_remote_copy(
        src_ref=others, dst_ref=others, send_sem=fac_send, recv_sem=fac_recv,
        device_id=col_peer[1], device_id_type=MESH,
    )
    fac_all.wait_recv()

    def facx_copy(source_x, d):
        return pltpu.make_async_remote_copy(
            src_ref=fbuf.at[source_x], dst_ref=fbuf.at[source_x], send_sem=facx_send.at[d],
            recv_sem=facx_recv.at[d], device_id=x_peer[d], device_id_type=MESH,
        )

    for d in range(1, nx):
        facx_copy(my_x, d).start()

    def spread_cond(k, l):
        return (k < cc) & (l // vc == k)

    def spread_val(k, l):
        return (k >= cc) & (k < cc + vc) & (l % vc == k - cc)

    def pairs(factors, entries):
        rows = entries * cf
        conds = mm(factors, one_hot((128, tc), spread_cond)).astype(BF16)
        vals = mm(factors, one_hot((128, tc), spread_val)).astype(BF16)
        left = mm(one_hot((entries * tf, rows), lambda t, k: t // vf == k), conds)
        right = mm(
            one_hot((entries * tf, rows), lambda t, k: (t // tf) * cf + t % vf == k), vals
        )
        return left * right

    fine_cols = col_cond.shape[0]
    ccond = col_cond[...].astype(F32).reshape(fine_cols * cf, cc).astype(BF16)
    cval = col_val[...].astype(F32)
    cval = jnp.concatenate([cval] * (cf // vf), axis=1).reshape(fine_cols * cf, vc).astype(BF16)
    cpacked = mm(ccond, one_hot((cc, 128), lambda k, l: l == k)) + mm(
        cval, one_hot((vc, 128), lambda k, l: l == k + cc)
    )
    right_pairs = pairs(cpacked.astype(BF16), fine_cols).T
    lane_point = jnp.zeros((1, width), jnp.int32)
    lane_f = lax.broadcasted_iota(jnp.int32, (1, width), 1) // tf
    for f in range(fine_cols):
        lane_point = jnp.where(lane_f == f, near_col[f], lane_point)
    for c in range(coarse.shape[1] // tc):
        smat[c * tc:(c + 1) * tc, :] = jnp.where(lane_point == c, right_pairs, 0.0).astype(BF16)

    for i in range(fine_rows):
        o = own_s[my_x * fine_rows + i]
        second = jnp.int32(0)
        for k in range(i):
            second = jnp.where(own_s[my_x * fine_rows + k] == o, 1, second)
        sel_s[i] = o * 2 + second

    def finish(z_src):
        o = my_x * nz + z_src
        work[...] = kbuf[z_src].reshape(work.shape)
        parts = []
        for d in range(nx):
            x = (my_x + d) % nx
            first, last = jnp.int32(0), jnp.int32(0)
            hits = []
            for i in range(fine_rows):
                hits.append((own_s[x * fine_rows + i] == o, enc_s[x * fine_rows + i]))
            for i in range(fine_rows):
                last = jnp.where(hits[i][0], hits[i][1], last)
                j = fine_rows - 1 - i
                first = jnp.where(hits[j][0], hits[j][1], first)
            for entry in (first, last):
                parts.append(mm(pbuf[x, entry >> shift], work[entry & (points - 1)]))
        partial = jnp.concatenate(parts, axis=0)
        high = partial.astype(BF16)
        low = (partial - high.astype(F32)).astype(BF16)
        done = (mm(high, smat[...]) + mm(low, smat[...])).astype(BF16)
        done = done.reshape(nx, 2, tf, width)
        ybuf[pl.ds(o * 2, 2)] = done[0]
        for d in range(1, nx):
            ysend[z_src, d - 1] = done[d]
            pltpu.make_async_remote_copy(
                src_ref=ysend.at[z_src, d - 1], dst_ref=ybuf.at[pl.ds(o * 2, 2)], send_sem=x_send,
                recv_sem=x_recv.at[d], device_id=x_peer[d], device_id_type=MESH,
            ).start()

    local.wait()
    for d in range(1, nx):
        facx_copy((my_x + nx - d) % nx, d).wait_recv()
    for x in range(nx):
        pbuf[x] = pairs(fbuf[x], fine_rows).astype(BF16).reshape(fine_rows, tf, tc)
    finish(my_z)

    def hop_step(hop, carry):
        for piece in range(points):
            for way in (0, 1):
                z_src = arrived(way, hop - 1)
                ring_copy(way, hop - 1, piece, z_src).wait_recv()
                ring_copy(way, hop, piece, z_src).start()
        for way in (0, 1):
            finish(arrived(way, hop - 1))
        return carry

    lax.fori_loop(2, half, hop_step, 0)
    for piece in range(points):
        for way in (0, 1):
            z_src = arrived(way, half - 1)
            ring_copy(way, half - 1, piece, z_src).wait_recv()
            if (piece < points // 2) == (way == 0):
                ring_copy(way, half, piece, z_src).start()
    for way in (0, 1):
        finish(arrived(way, half - 1))
    for piece in range(points):
        way = 0 if piece < points // 2 else 1
        ring_copy(way, half, piece, arrived(way, half)).wait_recv()
    finish(arrived(0, half))

    for d in range(1, nx):
        x = (my_x + nx - d) % nx
        block = ybuf.at[pl.ds(x * nz * 2, nz * 2)]
        pltpu.make_async_remote_copy(
            src_ref=block, dst_ref=block, send_sem=x_send, recv_sem=x_recv.at[d],
            device_id=x_peer[d], device_id_type=MESH,
        ).wait_recv()
    for i in range(fine_rows):
        out[i * tf:(i + 1) * tf, :] = ybuf[sel_s[i]]

    ring = kbuf.at[pl.ds(0, nz - 1)]
    pltpu.make_async_remote_copy(
        src_ref=ring, dst_ref=ring, send_sem=ring_send, recv_sem=ring_recv.at[0, 0, 0],
        device_id=z_up, device_id_type=MESH,
    ).wait_send()
    fac_all.wait_send()
    for d in range(1, nx):
        facx_copy(my_x, d).wait_send()
    pltpu.make_async_remote_copy(
        src_ref=ysend, dst_ref=ysend, send_sem=x_send, recv_sem=x_recv.at[0],
        device_id=x_peer[1], device_id_type=MESH,
    ).wait_send()


def shards(nx, nz, nc, coarse, row_cond, row_val, col_cond, col_val, near_row, owner_map, near_col):
    cf, cc = row_cond.shape[1:]
    vf, vc = row_val.shape[1:]
    tc, tf = cc * vc, cf * vf
    points = coarse.shape[0] // tc
    fine_rows = row_cond.shape[0] * nc
    width = col_cond.shape[0] * tf
    span = coarse.shape[1]
    return pl.pallas_call(
        functools.partial(kernel, nx, nz, nc, cf, vf, cc, vc),
        out_shape=jax.ShapeDtypeStruct((fine_rows * tf, width), BF16),
        in_specs=[pl.BlockSpec(memory_space=pltpu.HBM)] * 8,
        out_specs=pl.BlockSpec(memory_space=pltpu.VMEM),
        scratch_shapes=[
            pltpu.VMEM(row_cond.shape, BF16),
            pltpu.VMEM(row_val.shape, BF16),
            pltpu.VMEM(col_cond.shape, BF16),
            pltpu.VMEM(col_val.shape, BF16),
            pltpu.SMEM(near_row.shape, jnp.int32),
            pltpu.SMEM(owner_map.shape, jnp.int32),
            pltpu.SMEM(near_col.shape, jnp.int32),
            pltpu.VMEM((nz, points * tc, span), BF16),
            pltpu.VMEM((points, tc, span), BF16),
            pltpu.VMEM((nx, fine_rows * cf, 128), BF16),
            pltpu.VMEM((nx, fine_rows, tf, tc), BF16),
            pltpu.VMEM((span, width), BF16),
            pltpu.VMEM((nx * nz * 2, tf, width), BF16),
            pltpu.VMEM((nz, nx - 1, 2, tf, width), BF16),
            pltpu.SMEM((nx * fine_rows,), jnp.int32),
            pltpu.SMEM((nx * fine_rows,), jnp.int32),
            pltpu.SMEM((fine_rows,), jnp.int32),
            pltpu.SemaphoreType.DMA((2, nz // 2 + 1, points)),
            pltpu.SemaphoreType.DMA,
            pltpu.SemaphoreType.DMA((7,)),
            pltpu.SemaphoreType.DMA,
            pltpu.SemaphoreType.DMA,
            pltpu.SemaphoreType.DMA,
            pltpu.SemaphoreType.DMA((nx,)),
            pltpu.SemaphoreType.DMA((nx,)),
            pltpu.SemaphoreType.DMA((nx,)),
            pltpu.SemaphoreType.DMA,
        ],
        compiler_params=pltpu.CompilerParams(
            collective_id=0, has_side_effects=True, vmem_limit_bytes=60 * 1024 * 1024
        ),
    )(coarse, row_cond, row_val, col_cond, col_val, near_row, owner_map, near_col)


def solution(mesh, nz=Z_SIZE):
    nx, nc = mesh.shape["row"] // nz, mesh.shape["col"]
    return jax.shard_map(
        functools.partial(shards, nx, nz, nc),
        mesh=mesh,
        in_specs=(
            P("row", "col"),
            P(("row", "col"), None, None),
            P(("row", "col"), None, None),
            P("col", None, None),
            P("col", None, None),
            P(),
            P(),
            P("col"),
        ),
        out_specs=P("row", "col"),
        check_vma=False,
    )
```

```python
import functools

import jax
import jax.numpy as jnp
from jax import lax
from jax.experimental import pallas as pl
from jax.experimental.pallas import tpu as pltpu
from jax.sharding import PartitionSpec as P

MESH = pl.DeviceIdType.MESH
F32 = jnp.float32
BF16 = jnp.bfloat16
Z_SIZE = 16


def one_hot(shape, test):
    rows = lax.broadcasted_iota(jnp.int32, shape, 0)
    lanes = lax.broadcasted_iota(jnp.int32, shape, 1)
    return jnp.where(test(rows, lanes), 1.0, 0.0).astype(BF16)


def mm(a, b):
    return jnp.dot(a, b, preferred_element_type=F32)


def kernel(
    nx, nz, nc, cf, vf, cc, vc,
    coarse, row_cond_in, row_val_in, col_cond_in, col_val_in, near_row_in, owner_map_in, near_col_in,
    out,
    row_cond, row_val, col_cond, col_val, near_row, owner_map, near_col,
    kbuf, work_0, work_1, fbuf, pbuf, pfar, lane_pat, row_pat, pick, smat, ybuf, ysend, yfar,
    own_s, enc_s, sel_s, found,
    ring_recv, ring_send, fetch_sem, local_sem, fac_recv, fac_send, x_recv, x_send, far_recv, far_send,
):
    me = lax.axis_index("row")
    my_col = lax.axis_index("col")
    my_x, my_z = me // nz, me % nz
    reach = nz // 2 - 2
    near = (-2, -1, 1, 2)
    groups = nx * (1 + len(near))
    tc, tf = cc * vc, cf * vf
    points = coarse.shape[0] // tc
    shift = points.bit_length() - 1
    assert points == 1 << shift
    fine_rows = out.shape[0] // tf
    width = out.shape[1]
    my_rows = row_cond.shape[0]
    row_shift = my_rows.bit_length() - 1
    assert my_rows == 1 << row_shift
    fac_rows = my_rows * cf

    z_up = (my_x * nz + (my_z + 1) % nz, my_col)
    z_down = (my_x * nz + (my_z + nz - 1) % nz, my_col)
    x_peer = [(((my_x + d) % nx) * nz + my_z, my_col) for d in range(nx)]
    col_peer = [(me, (my_col + d) % nc) for d in range(nc)]
    layer_peer = {
        dz: [(((my_x + d) % nx) * nz + (my_z + dz + nz) % nz, my_col) for d in range(nx)]
        for dz in near
    }

    barrier = pltpu.get_barrier_semaphore()
    peers = sum(layer_peer.values(), []) + x_peer[1:] + col_peer[1:]
    for peer in peers:
        pl.semaphore_signal(barrier, inc=1, device_id=peer, device_id_type=MESH)

    fetches = [
        pltpu.make_async_copy(source, target, fetch_sem.at[k])
        for k, (source, target) in enumerate((
            (row_cond_in, row_cond), (row_val_in, row_val), (near_row_in, near_row),
            (owner_map_in, owner_map), (near_col_in, near_col), (col_cond_in, col_cond),
            (col_val_in, col_val),
        ))
    ]
    for fetch in fetches:
        fetch.start()
    local = pltpu.make_async_copy(coarse, kbuf.at[my_z], local_sem)
    local.start()
    pl.semaphore_wait(barrier, len(peers))

    def ring_copy(way, hop, piece, src, first=False):
        rows = pl.ds(piece * tc, tc)
        source = coarse.at[rows, :] if first else kbuf.at[src, rows, :]
        return pltpu.make_async_remote_copy(
            src_ref=source,
            dst_ref=kbuf.at[src, rows, :],
            send_sem=ring_send,
            recv_sem=ring_recv.at[way, hop, piece],
            device_id=z_up if way == 0 else z_down,
            device_id_type=MESH,
        )

    def arrived(way, hop):
        return (my_z + nz - hop) % nz if way == 0 else (my_z + hop) % nz

    for piece in range(points):
        for way in (0, 1):
            ring_copy(way, 1, piece, my_z, first=True).start()

    for fetch in fetches[:2]:
        fetch.wait()
    cond = row_cond[...].astype(F32).reshape(fac_rows, cc).astype(BF16)
    val = row_val[...].astype(F32)
    val = jnp.concatenate([val] * (cf // vf), axis=1).reshape(fac_rows, vc).astype(BF16)
    packed = mm(cond, one_hot((cc, 128), lambda k, l: l == k)) + mm(
        val, one_hot((vc, 128), lambda k, l: l == k + cc)
    )
    fbuf[my_col, my_x] = packed.astype(BF16)
    def move(src, dst, send, recv, peer):
        return pltpu.make_async_remote_copy(
            src_ref=src, dst_ref=dst, send_sem=send, recv_sem=recv, device_id=peer, device_id_type=MESH
        )

    mine = fbuf.at[my_col, my_x]
    for d in range(1, nx):
        move(mine, mine, fac_send, fac_recv.at[0], x_peer[d]).start()
    for dz in near:
        there = fbuf.at[my_col, nx + my_x * len(near) + near.index(-dz)]
        move(mine, there, fac_send, fac_recv.at[1], layer_peer[dz][0]).start()

    def group_place(g):
        far = (g - nx) % len(near)
        dz = far - 2 + jnp.where(far >= 2, 1, 0)
        x = jnp.where(g < nx, g, (g - nx) // len(near))
        return x, (my_z + jnp.where(g < nx, 0, dz) + nz) % nz

    def list_group(g):
        x, z = group_place(g)
        for i in range(fine_rows):
            slot = owner_map[near_row[(x * nz + z) * fine_rows + i]]
            own_s[g * fine_rows + i] = slot >> shift
            enc_s[g * fine_rows + i] = (i << shift) + (slot & (points - 1))

    def list_groups(start, count):
        def one(g, carry):
            list_group(g)
            return carry

        lax.fori_loop(start, start + count, one, 0)

    far_count = nx * len(near)
    layer_tiles = fbuf.at[my_col, pl.ds(0, nx)]
    near_tiles = fbuf.at[my_col, pl.ds(nx + my_x * len(near), len(near))]
    far_tiles = fbuf.at[my_col, pl.ds(nx, far_count)]

    def pass_layer_tiles():
        got = fbuf.at[my_col, pl.ds(0, nx - 1)]
        move(got, got, fac_send, fac_recv.at[0], x_peer[1]).wait_recv()
        for d in range(1, nc):
            move(layer_tiles, layer_tiles, fac_send, fac_recv.at[2], col_peer[d]).start()
        move(near_tiles, near_tiles, fac_send, fac_recv.at[1], z_up).wait_recv()
        for d in range(1, nx):
            move(near_tiles, near_tiles, fac_send, fac_recv.at[3], x_peer[d]).start()

    def pass_far_tiles():
        got = fbuf.at[my_col, pl.ds(nx, far_count - len(near))]
        move(got, got, fac_send, fac_recv.at[3], x_peer[1]).wait_recv()
        for d in range(1, nc):
            move(far_tiles, far_tiles, fac_send, fac_recv.at[4], col_peer[d]).start()

    def make_patterns():
        lane_pat[0] = one_hot((128, tc), lambda k, l: (k < cc) & (l // vc == k))
        lane_pat[1] = one_hot(
            (128, tc), lambda k, l: (k >= cc) & (k < cc + vc) & (l % vc == k - cc)
        )
        shape = row_pat.shape[1:]
        row_pat[0] = one_hot(shape, lambda t, k: t // vf == k)
        row_pat[1] = one_hot(shape, lambda t, k: (t // tf) * cf + t % vf == k)
        for row in range(my_rows):
            pick[row] = one_hot((tf, fac_rows), lambda t, k: k == row * cf + t // vf)
            pick[my_rows + row] = one_hot((tf, fac_rows), lambda t, k: k == row * cf + t % vf)

    def pairs(factors, entries):
        rows = entries * cf
        conds = mm(factors, lane_pat[0]).astype(BF16)
        vals = mm(factors, lane_pat[1]).astype(BF16)
        left = mm(row_pat[0, :entries * tf, :rows], conds)
        return left * mm(row_pat[1, :entries * tf, :rows], vals)

    def make_smat():
        fine_cols = col_cond.shape[0]
        ccond = col_cond[...].astype(F32).reshape(fine_cols * cf, cc).astype(BF16)
        cval = col_val[...].astype(F32)
        cval = jnp.concatenate([cval] * (cf // vf), axis=1)
        cval = cval.reshape(fine_cols * cf, vc).astype(BF16)
        cpacked = mm(ccond, one_hot((cc, 128), lambda k, l: l == k)) + mm(
            cval, one_hot((vc, 128), lambda k, l: l == k + cc)
        )
        right_pairs = pairs(cpacked.astype(BF16), fine_cols).T
        lane_point = jnp.zeros((1, width), jnp.int32)
        lane_f = lax.broadcasted_iota(jnp.int32, (1, width), 1) // tf
        for f in range(fine_cols):
            lane_point = jnp.where(lane_f == f, near_col[f], lane_point)
        for c in range(coarse.shape[1] // tc):
            smat[c * tc:(c + 1) * tc, :] = jnp.where(
                lane_point == c, right_pairs, 0.0
            ).astype(BF16)

    def make_sel():
        for i in range(fine_rows):
            o = own_s[my_x * fine_rows + i]
            second = jnp.int32(0)
            for k in range(i):
                second = jnp.where(own_s[my_x * fine_rows + k] == o, 1, second)
            sel_s[i] = o * 2 + second

    def find(z_src, k, group_of):
        o = my_x * nz + z_src
        for d in range(nx):
            base = group_of((my_x + d) % nx) * fine_rows
            first, last = jnp.int32(0), jnp.int32(0)
            hits = [(own_s[base + i] == o, enc_s[base + i]) for i in range(fine_rows)]
            for i in range(fine_rows):
                last = jnp.where(hits[i][0], hits[i][1], last)
                j = fine_rows - 1 - i
                first = jnp.where(hits[j][0], hits[j][1], first)
            found[k, 2 * d] = first
            found[k, 2 * d + 1] = last

    def rows_of(work, k, d, slots, pair):
        parts = []
        for slot in slots:
            entry = found[k, 2 * d + slot]
            parts.append(mm(pair(entry, slot), work[entry & (points - 1)]))
        partial = parts[0] if len(parts) == 1 else jnp.concatenate(parts, axis=0)
        done = mm(partial.astype(BF16), smat[...]).astype(BF16)
        return done.reshape(len(slots), tf, width)

    def load(work, z_src):
        work[...] = kbuf[z_src].reshape(work.shape)

    works = (work_0, work_1)

    def own_group(x):
        return x

    def finish(work, z_src, k):
        o = my_x * nz + z_src
        for d in [*range(1, nx), 0]:
            group = (my_x + d) % nx
            done = rows_of(work, k, d, (0, 1), lambda entry, slot: pbuf[group, entry >> shift])
            if d == 0:
                ybuf[pl.ds(o * 2, 2)] = done
                continue
            ysend[z_src, d - 1] = done
            move(
                ysend.at[z_src, d - 1], ybuf.at[pl.ds(o * 2, 2)], x_send, x_recv.at[d], x_peer[d]
            ).start()

    def finish_far(work, z_src, k, dz, slots, place):
        o = my_x * nz + z_src
        for d in range(nx):
            at = place + d * len(slots)
            yfar[at:at + len(slots)] = rows_of(
                work, k, d, slots, lambda entry, slot: pfar[at + slot - slots[0]]
            )
            move(
                yfar.at[pl.ds(at, len(slots))], ybuf.at[pl.ds(o * 2 + slots[0], len(slots))],
                far_send, far_recv, layer_peer[dz][d],
            ).start()

    def far_pairs(k, dz, slots, place):
        left, right = [], []
        for d in range(nx):
            group = nx + ((my_x + d) % nx) * len(near) + near.index(dz)
            for slot in slots:
                row = found[k, 2 * d + slot] >> shift
                tile = fbuf[row >> row_shift, group]
                row = row & (my_rows - 1)
                left.append(mm(pick[row], tile).astype(BF16))
                right.append(mm(pick[my_rows + row], tile).astype(BF16))
        product = mm(jnp.concatenate(left, axis=0), lane_pat[0]) * mm(
            jnp.concatenate(right, axis=0), lane_pat[1]
        )
        pfar[place:place + nx * len(slots)] = product.astype(BF16).reshape(-1, tf, tc)

    def forward(hop, piece):
        for way in (0, 1):
            z_src = arrived(way, hop - 1)
            ring_copy(way, hop - 1, piece, z_src).wait_recv()
            ring_copy(way, hop, piece, z_src).start()

    def near_group(dz):
        return lambda x: nx + x * len(near) + near.index(dz)

    def first_lists():
        for fetch in fetches[2:]:
            fetch.wait()
        list_groups(0, nx)
        make_sel()
        find(my_z, 0, own_group)

    def first_matrices():
        make_patterns()
        make_smat()

    beside = [pass_layer_tiles, first_matrices, local.wait]
    first_lists()
    for piece in range(points):
        forward(2, piece)
        if piece < len(beside):
            beside[piece]()
    got = fbuf.at[pl.ds(0, nc - 1), pl.ds(0, nx)]
    move(got, got, fac_send, fac_recv.at[2], col_peer[1]).wait_recv()
    for g in range(nx):
        factors = fbuf[:, g].reshape(nc * fac_rows, 128)
        pbuf[g] = pairs(factors, fine_rows).astype(BF16).reshape(fine_rows, tf, tc)
    load(work_0, my_z)
    finish(work_0, my_z, 0)
    for way in (0, 1):
        find(arrived(way, 1), way, own_group)
    pass_far_tiles()

    share = -(-far_count // (reach - 2))

    def hop_step(hop, carry):
        start = nx + (hop - 3) * share
        count = jnp.minimum(share, groups - start)
        for piece in range(points):
            forward(hop, piece)
            if piece < 2:
                load(works[piece], arrived(piece, hop - 2))
                finish(works[piece], arrived(piece, hop - 2), piece)
            elif piece == 2:
                list_groups(start, count)
        for way in (0, 1):
            find(arrived(way, hop - 1), way, own_group)
        return carry

    lax.fori_loop(3, reach + 1, hop_step, 0)
    for way in (0, 1):
        load(works[way], arrived(way, reach - 1))
        finish(works[way], arrived(way, reach - 1), way)
    got = fbuf.at[pl.ds(0, nc - 1), pl.ds(nx, far_count)]
    move(got, got, fac_send, fac_recv.at[4], col_peer[1]).wait_recv()
    per = nx * 3
    sides = ((0, 1), (1, -1))
    for way, sign in sides:
        z_src = arrived(way, reach)
        find(z_src, 2 + way, near_group(2 * sign))
        find(z_src, 4 + way, near_group(sign))
        far_pairs(2 + way, 2 * sign, (way,), way * per)
        far_pairs(4 + way, sign, (0, 1), way * per + nx)
        find(z_src, way, own_group)
    for way, sign in sides:
        z_src = arrived(way, reach)
        for piece in range(points):
            ring_copy(way, reach, piece, z_src).wait_recv()
        load(works[way], z_src)
        finish_far(works[way], z_src, 2 + way, 2 * sign, (way,), way * per)
        finish_far(works[way], z_src, 4 + way, sign, (0, 1), way * per + nx)
        finish(works[way], z_src, way)

    for d in range(1, nx):
        block = ybuf.at[pl.ds(0, (2 * reach + 1) * 2)]
        move(block, block, x_send, x_recv.at[d], x_peer[d]).wait_recv()
    block = ybuf.at[pl.ds(0, 2 * per)]
    move(block, block, far_send, far_recv, x_peer[1]).wait_recv()
    for i in range(fine_rows):
        out[i * tf:(i + 1) * tf, :] = ybuf[sel_s[i]]

    move(block, block, far_send, far_recv, x_peer[1]).wait_send()
    ring = kbuf.at[pl.ds(0, 2 * reach)]
    move(ring, ring, ring_send, ring_recv.at[0, 0, 0], z_up).wait_send()
    block = ysend.at[pl.ds(0, 2 * reach + 1)]
    move(block, block, x_send, x_recv.at[0], x_peer[1]).wait_send()
    for sent in (
        fbuf.at[0, pl.ds(0, nx - 1)], fbuf.at[0, pl.ds(0, len(near))],
        fbuf.at[pl.ds(0, nc - 1), pl.ds(0, nx)], fbuf.at[pl.ds(0, nx - 1), pl.ds(0, len(near))],
        fbuf.at[pl.ds(0, nc - 1), pl.ds(nx, far_count)],
    ):
        move(sent, sent, fac_send, fac_recv.at[0], x_peer[1]).wait_send()


def shards(nx, nz, nc, coarse, row_cond, row_val, col_cond, col_val, near_row, owner_map, near_col):
    cf, cc = row_cond.shape[1:]
    vf, vc = row_val.shape[1:]
    tc, tf = cc * vc, cf * vf
    points = coarse.shape[0] // tc
    fine_rows = row_cond.shape[0] * nc
    width = col_cond.shape[0] * tf
    groups = nx * 5
    span = coarse.shape[1]
    return pl.pallas_call(
        functools.partial(kernel, nx, nz, nc, cf, vf, cc, vc),
        out_shape=pltpu.VMEM((fine_rows * tf, width), BF16),
        in_specs=[pl.BlockSpec(memory_space=pltpu.HBM)] * 8,
        out_specs=pl.BlockSpec(memory_space=pltpu.VMEM),
        scratch_shapes=[
            pltpu.VMEM(row_cond.shape, BF16),
            pltpu.VMEM(row_val.shape, BF16),
            pltpu.VMEM(col_cond.shape, BF16),
            pltpu.VMEM(col_val.shape, BF16),
            pltpu.SMEM(near_row.shape, jnp.int32),
            pltpu.SMEM(owner_map.shape, jnp.int32),
            pltpu.SMEM(near_col.shape, jnp.int32),
            pltpu.VMEM((nz, points * tc, span), BF16),
            pltpu.VMEM((points, tc, span), BF16),
            pltpu.VMEM((points, tc, span), BF16),
            pltpu.VMEM((nc, groups, row_cond.shape[0] * cf, 128), BF16),
            pltpu.VMEM((nx, fine_rows, tf, tc), BF16),
            pltpu.VMEM((nx * 6, tf, tc), BF16),
            pltpu.VMEM((2, 128, tc), BF16),
            pltpu.VMEM((2, fine_rows * tf, fine_rows * cf), BF16),
            pltpu.VMEM((2 * row_cond.shape[0], tf, row_cond.shape[0] * cf), BF16),
            pltpu.VMEM((span, width), BF16),
            pltpu.VMEM((nx * nz * 2, tf, width), BF16),
            pltpu.VMEM((nz, nx - 1, 2, tf, width), BF16),
            pltpu.VMEM((nx * 6, tf, width), BF16),
            pltpu.SMEM((groups * fine_rows,), jnp.int32),
            pltpu.SMEM((groups * fine_rows,), jnp.int32),
            pltpu.SMEM((fine_rows,), jnp.int32),
            pltpu.SMEM((6, 2 * nx), jnp.int32),
            pltpu.SemaphoreType.DMA((2, nz // 2 + 1, points)),
            pltpu.SemaphoreType.DMA,
            pltpu.SemaphoreType.DMA((7,)),
            pltpu.SemaphoreType.DMA,
            pltpu.SemaphoreType.DMA((5,)),
            pltpu.SemaphoreType.DMA,
            pltpu.SemaphoreType.DMA((nx,)),
            pltpu.SemaphoreType.DMA,
            pltpu.SemaphoreType.DMA,
            pltpu.SemaphoreType.DMA,
        ],
        compiler_params=pltpu.CompilerParams(
            collective_id=0, has_side_effects=True, vmem_limit_bytes=60 * 1024 * 1024
        ),
    )(coarse, row_cond, row_val, col_cond, col_val, near_row, owner_map, near_col)


def solution(mesh, nz=Z_SIZE):
    nx, nc = mesh.shape["row"] // nz, mesh.shape["col"]
    return jax.shard_map(
        functools.partial(shards, nx, nz, nc),
        mesh=mesh,
        in_specs=(
            P("row", "col"),
            P(("row", "col"), None, None),
            P(("row", "col"), None, None),
            P("col", None, None),
            P("col", None, None),
            P(),
            P(),
            P("col"),
        ),
        out_specs=P("row", "col"),
        check_vma=False,
    )
```

```python
import functools

import jax
import jax.numpy as jnp
from jax import lax
from jax.experimental import pallas as pl
from jax.experimental.pallas import tpu as pltpu
from jax.sharding import PartitionSpec as P

MESH = pl.DeviceIdType.MESH
F32 = jnp.float32
BF16 = jnp.bfloat16
Z_SIZE = 16


def one_hot(shape, test):
    rows = lax.broadcasted_iota(jnp.int32, shape, 0)
    lanes = lax.broadcasted_iota(jnp.int32, shape, 1)
    return jnp.where(test(rows, lanes), 1.0, 0.0).astype(BF16)


def mm(a, b):
    return jnp.dot(a, b, preferred_element_type=F32)


def kernel(
    nx, nz, nc, cf, vf, cc, vc,
    coarse, row_cond_in, row_val_in, col_cond_in, col_val_in, near_row_in, owner_map_in, near_col_in,
    out,
    row_cond, row_val, col_cond, col_val, near_row, owner_map, near_col,
    kbuf, own_left, far_left, fbuf, pbuf, lane_pat, row_pat, pick, smat, ybuf, ysend, yfar,
    own_s, enc_s, sel_s, found,
    ring_recv, ring_send, fetch_sem, local_sem, fac_recv, fac_send, x_recv, x_send, far_recv, far_send,
):
    me = lax.axis_index("row")
    my_col = lax.axis_index("col")
    my_x, my_z = me // nz, me % nz
    reach = nz // 2 - 2
    near = (-2, -1, 1, 2)
    groups = nx * (1 + len(near))
    tc, tf = cc * vc, cf * vf
    points = coarse.shape[0] // tc
    shift = points.bit_length() - 1
    assert points == 1 << shift
    fine_rows = out.shape[0] // tf
    width = out.shape[1]
    my_rows = row_cond.shape[0]
    row_shift = my_rows.bit_length() - 1
    assert my_rows == 1 << row_shift
    fac_rows = my_rows * cf

    z_up = (my_x * nz + (my_z + 1) % nz, my_col)
    z_down = (my_x * nz + (my_z + nz - 1) % nz, my_col)
    x_peer = [(((my_x + d) % nx) * nz + my_z, my_col) for d in range(nx)]
    col_peer = [(me, (my_col + d) % nc) for d in range(nc)]
    layer_peer = {
        dz: [(((my_x + d) % nx) * nz + (my_z + dz + nz) % nz, my_col) for d in range(nx)]
        for dz in near
    }

    barrier = pltpu.get_barrier_semaphore()
    peers = sum(layer_peer.values(), []) + x_peer[1:] + col_peer[1:]
    for peer in peers:
        pl.semaphore_signal(barrier, inc=1, device_id=peer, device_id_type=MESH)

    fetches = [
        pltpu.make_async_copy(source, target, fetch_sem.at[k])
        for k, (source, target) in enumerate((
            (row_cond_in, row_cond), (row_val_in, row_val), (near_row_in, near_row),
            (owner_map_in, owner_map), (near_col_in, near_col), (col_cond_in, col_cond),
            (col_val_in, col_val),
        ))
    ]
    for fetch in fetches:
        fetch.start()
    local = pltpu.make_async_copy(coarse, kbuf.at[my_z], local_sem)
    local.start()
    pl.semaphore_wait(barrier, len(peers))

    def ring_copy(way, hop, piece, src, first=False):
        rows = pl.ds(piece * tc, tc)
        source = coarse.at[rows, :] if first else kbuf.at[src, rows, :]
        return pltpu.make_async_remote_copy(
            src_ref=source,
            dst_ref=kbuf.at[src, rows, :],
            send_sem=ring_send,
            recv_sem=ring_recv.at[way, hop, piece],
            device_id=z_up if way == 0 else z_down,
            device_id_type=MESH,
        )

    def arrived(way, hop):
        return (my_z + nz - hop) % nz if way == 0 else (my_z + hop) % nz

    for piece in range(points):
        for way in (0, 1):
            ring_copy(way, 1, piece, my_z, first=True).start()

    for fetch in fetches[:2]:
        fetch.wait()
    cond = row_cond[...].astype(F32).reshape(fac_rows, cc).astype(BF16)
    val = row_val[...].astype(F32)
    val = jnp.concatenate([val] * (cf // vf), axis=1).reshape(fac_rows, vc).astype(BF16)
    packed = mm(cond, one_hot((cc, 128), lambda k, l: l == k)) + mm(
        val, one_hot((vc, 128), lambda k, l: l == k + cc)
    )
    fbuf[my_col, my_x] = packed.astype(BF16)
    def move(src, dst, send, recv, peer):
        return pltpu.make_async_remote_copy(
            src_ref=src, dst_ref=dst, send_sem=send, recv_sem=recv, device_id=peer, device_id_type=MESH
        )

    mine = fbuf.at[my_col, my_x]
    for d in range(1, nx):
        move(mine, mine, fac_send, fac_recv.at[0], x_peer[d]).start()
    for dz in near:
        there = fbuf.at[my_col, nx + my_x * len(near) + near.index(-dz)]
        move(mine, there, fac_send, fac_recv.at[1], layer_peer[dz][0]).start()

    def group_place(g):
        far = (g - nx) % len(near)
        dz = far - 2 + jnp.where(far >= 2, 1, 0)
        x = jnp.where(g < nx, g, (g - nx) // len(near))
        return x, (my_z + jnp.where(g < nx, 0, dz) + nz) % nz

    def list_group(g):
        x, z = group_place(g)
        for i in range(fine_rows):
            slot = owner_map[near_row[(x * nz + z) * fine_rows + i]]
            own_s[g * fine_rows + i] = slot >> shift
            enc_s[g * fine_rows + i] = (i << shift) + (slot & (points - 1))

    def list_groups(start, count):
        def one(g, carry):
            list_group(g)
            return carry

        lax.fori_loop(start, start + count, one, 0)

    far_count = nx * len(near)
    layer_tiles = fbuf.at[my_col, pl.ds(0, nx)]
    near_tiles = fbuf.at[my_col, pl.ds(nx + my_x * len(near), len(near))]
    far_tiles = fbuf.at[my_col, pl.ds(nx, far_count)]

    def pass_layer_tiles():
        got = fbuf.at[my_col, pl.ds(0, nx - 1)]
        move(got, got, fac_send, fac_recv.at[0], x_peer[1]).wait_recv()
        for d in range(1, nc):
            move(layer_tiles, layer_tiles, fac_send, fac_recv.at[2], col_peer[d]).start()
        move(near_tiles, near_tiles, fac_send, fac_recv.at[1], z_up).wait_recv()
        for d in range(1, nx):
            move(near_tiles, near_tiles, fac_send, fac_recv.at[3], x_peer[d]).start()

    def pass_far_tiles():
        got = fbuf.at[my_col, pl.ds(nx, far_count - len(near))]
        move(got, got, fac_send, fac_recv.at[3], x_peer[1]).wait_recv()
        for d in range(1, nc):
            move(far_tiles, far_tiles, fac_send, fac_recv.at[4], col_peer[d]).start()

    def make_patterns():
        lane_pat[0] = one_hot((128, tc), lambda k, l: (k < cc) & (l // vc == k))
        lane_pat[1] = one_hot(
            (128, tc), lambda k, l: (k >= cc) & (k < cc + vc) & (l % vc == k - cc)
        )
        shape = row_pat.shape[1:]
        row_pat[0] = one_hot(shape, lambda t, k: t // vf == k)
        row_pat[1] = one_hot(shape, lambda t, k: (t // tf) * cf + t % vf == k)
        for row in range(my_rows):
            pick[row] = one_hot((tf, fac_rows), lambda t, k: k == row * cf + t // vf)
            pick[my_rows + row] = one_hot((tf, fac_rows), lambda t, k: k == row * cf + t % vf)

    def pairs(factors, entries):
        rows = entries * cf
        conds = mm(factors, lane_pat[0]).astype(BF16)
        vals = mm(factors, lane_pat[1]).astype(BF16)
        left = mm(row_pat[0, :entries * tf, :rows], conds)
        return left * mm(row_pat[1, :entries * tf, :rows], vals)

    def make_smat():
        fine_cols = col_cond.shape[0]
        ccond = col_cond[...].astype(F32).reshape(fine_cols * cf, cc).astype(BF16)
        cval = col_val[...].astype(F32)
        cval = jnp.concatenate([cval] * (cf // vf), axis=1)
        cval = cval.reshape(fine_cols * cf, vc).astype(BF16)
        cpacked = mm(ccond, one_hot((cc, 128), lambda k, l: l == k)) + mm(
            cval, one_hot((vc, 128), lambda k, l: l == k + cc)
        )
        right_pairs = pairs(cpacked.astype(BF16), fine_cols).T
        lane_point = jnp.zeros((1, width), jnp.int32)
        lane_f = lax.broadcasted_iota(jnp.int32, (1, width), 1) // tf
        for f in range(fine_cols):
            lane_point = jnp.where(lane_f == f, near_col[f], lane_point)
        for c in range(coarse.shape[1] // tc):
            smat[c * tc:(c + 1) * tc, :] = jnp.where(
                lane_point == c, right_pairs, 0.0
            ).astype(BF16)

    def make_sel():
        for i in range(fine_rows):
            o = own_s[my_x * fine_rows + i]
            second = jnp.int32(0)
            for k in range(i):
                second = jnp.where(own_s[my_x * fine_rows + k] == o, 1, second)
            sel_s[i] = o * 2 + second

    def find(z_src, k, group_of):
        o = my_x * nz + z_src
        for d in range(nx):
            base = group_of((my_x + d) % nx) * fine_rows
            first, last = jnp.int32(0), jnp.int32(0)
            hits = [(own_s[base + i] == o, enc_s[base + i]) for i in range(fine_rows)]
            for i in range(fine_rows):
                last = jnp.where(hits[i][0], hits[i][1], last)
                j = fine_rows - 1 - i
                first = jnp.where(hits[j][0], hits[j][1], first)
            found[k, 2 * d] = first
            found[k, 2 * d + 1] = last

    def own_group(x):
        return x

    def place_pair(left, way, at, entry, pair):
        point = entry & (points - 1)
        for p in range(points):
            left[way, at * tf:(at + 1) * tf, p * tc:(p + 1) * tc] = jnp.where(point == p, pair, 0)

    def prepare(z_src, way):
        find(z_src, way, own_group)
        for d in range(nx):
            for slot in range(2):
                entry = found[way, 2 * d + slot]
                pair = pbuf[(my_x + d) % nx, entry >> shift]
                place_pair(own_left, way, 2 * d + slot, entry, pair)

    def contract(left, z_src):
        partial = mm(left, kbuf[z_src]).astype(BF16)
        return mm(partial, smat[...]).astype(BF16).reshape(-1, tf, width)

    def finish(z_src, way):
        o = my_x * nz + z_src
        done = contract(own_left[way], z_src)
        for d in [*range(1, nx), 0]:
            rows = done[2 * d:2 * d + 2]
            if d == 0:
                ybuf[pl.ds(o * 2, 2)] = rows
                continue
            ysend[z_src, d - 1] = rows
            move(
                ysend.at[z_src, d - 1], ybuf.at[pl.ds(o * 2, 2)], x_send, x_recv.at[d], x_peer[d]
            ).start()

    def finish_far(z_src, way, sign):
        o = my_x * nz + z_src
        place = way * nx * 3
        yfar[place:place + nx * 3] = contract(far_left[way], z_src)
        for dz, slots, at in ((2 * sign, (way,), place), (sign, (0, 1), place + nx)):
            for d in range(nx):
                move(
                    yfar.at[pl.ds(at + d * len(slots), len(slots))],
                    ybuf.at[pl.ds(o * 2 + slots[0], len(slots))],
                    far_send, far_recv, layer_peer[dz][d],
                ).start()

    def prepare_far(way, sign):
        left, right, entries = [], [], []
        z_src = arrived(way, reach)
        for k, dz, slots in ((2, 2 * sign, (way,)), (3, sign, (0, 1))):
            find(z_src, k, lambda x: nx + x * len(near) + near.index(dz))
            for d in range(nx):
                group = nx + ((my_x + d) % nx) * len(near) + near.index(dz)
                for slot in slots:
                    entry = found[k, 2 * d + slot]
                    row = entry >> shift
                    tile = fbuf[row >> row_shift, group]
                    row = row & (my_rows - 1)
                    entries.append(entry)
                    left.append(mm(pick[row], tile).astype(BF16))
                    right.append(mm(pick[my_rows + row], tile).astype(BF16))
        product = mm(jnp.concatenate(left, axis=0), lane_pat[0]) * mm(
            jnp.concatenate(right, axis=0), lane_pat[1]
        )
        product = product.astype(BF16)
        for at, entry in enumerate(entries):
            place_pair(far_left, way, at, entry, product[at * tf:(at + 1) * tf])

    def forward(hop, piece):
        for way in (0, 1):
            z_src = arrived(way, hop - 1)
            ring_copy(way, hop - 1, piece, z_src).wait_recv()
            ring_copy(way, hop, piece, z_src).start()

    def first_lists():
        for fetch in fetches[2:]:
            fetch.wait()
        list_groups(0, nx)
        make_sel()

    def first_matrices():
        make_patterns()
        make_smat()

    beside = [pass_layer_tiles, first_matrices, local.wait]
    first_lists()
    for piece in range(points):
        forward(2, piece)
        if piece < len(beside):
            beside[piece]()
    got = fbuf.at[pl.ds(0, nc - 1), pl.ds(0, nx)]
    move(got, got, fac_send, fac_recv.at[2], col_peer[1]).wait_recv()
    for g in range(nx):
        factors = fbuf[:, g].reshape(nc * fac_rows, 128)
        pbuf[g] = pairs(factors, fine_rows).astype(BF16).reshape(fine_rows, tf, tc)
    prepare(my_z, 0)
    finish(my_z, 0)
    for way in (0, 1):
        prepare(arrived(way, 1), way)
    pass_far_tiles()

    share = -(-far_count // (reach - 2))

    def hop_step(hop, carry):
        start = nx + (hop - 3) * share
        count = jnp.minimum(share, groups - start)
        for piece in range(points):
            forward(hop, piece)
            if piece < 2:
                finish(arrived(piece, hop - 2), piece)
            elif piece == 2:
                list_groups(start, count)
        for way in (0, 1):
            prepare(arrived(way, hop - 1), way)
        return carry

    lax.fori_loop(3, reach + 1, hop_step, 0)
    for way in (0, 1):
        finish(arrived(way, reach - 1), way)
    got = fbuf.at[pl.ds(0, nc - 1), pl.ds(nx, far_count)]
    move(got, got, fac_send, fac_recv.at[4], col_peer[1]).wait_recv()
    sides = ((0, 1), (1, -1))
    for way, sign in sides:
        prepare_far(way, sign)
        prepare(arrived(way, reach), way)
    for way, sign in sides:
        z_src = arrived(way, reach)
        for piece in range(points):
            ring_copy(way, reach, piece, z_src).wait_recv()
        finish_far(z_src, way, sign)
        finish(z_src, way)

    for d in range(1, nx):
        block = ybuf.at[pl.ds(0, (2 * reach + 1) * 2)]
        move(block, block, x_send, x_recv.at[d], x_peer[d]).wait_recv()
    block = ybuf.at[pl.ds(0, nx * 6)]
    move(block, block, far_send, far_recv, x_peer[1]).wait_recv()
    for i in range(fine_rows):
        out[i * tf:(i + 1) * tf, :] = ybuf[sel_s[i]]

    move(block, block, far_send, far_recv, x_peer[1]).wait_send()
    ring = kbuf.at[pl.ds(0, 2 * reach)]
    move(ring, ring, ring_send, ring_recv.at[0, 0, 0], z_up).wait_send()
    block = ysend.at[pl.ds(0, 2 * reach + 1)]
    move(block, block, x_send, x_recv.at[0], x_peer[1]).wait_send()
    for sent in (
        fbuf.at[0, pl.ds(0, nx - 1)], fbuf.at[0, pl.ds(0, len(near))],
        fbuf.at[pl.ds(0, nc - 1), pl.ds(0, nx)], fbuf.at[pl.ds(0, nx - 1), pl.ds(0, len(near))],
        fbuf.at[pl.ds(0, nc - 1), pl.ds(nx, far_count)],
    ):
        move(sent, sent, fac_send, fac_recv.at[0], x_peer[1]).wait_send()


def shards(nx, nz, nc, coarse, row_cond, row_val, col_cond, col_val, near_row, owner_map, near_col):
    cf, cc = row_cond.shape[1:]
    vf, vc = row_val.shape[1:]
    tc, tf = cc * vc, cf * vf
    points = coarse.shape[0] // tc
    fine_rows = row_cond.shape[0] * nc
    width = col_cond.shape[0] * tf
    groups = nx * 5
    span = coarse.shape[1]
    return pl.pallas_call(
        functools.partial(kernel, nx, nz, nc, cf, vf, cc, vc),
        out_shape=pltpu.VMEM((fine_rows * tf, width), BF16),
        in_specs=[pl.BlockSpec(memory_space=pltpu.HBM)] * 8,
        out_specs=pl.BlockSpec(memory_space=pltpu.VMEM),
        scratch_shapes=[
            pltpu.VMEM(row_cond.shape, BF16),
            pltpu.VMEM(row_val.shape, BF16),
            pltpu.VMEM(col_cond.shape, BF16),
            pltpu.VMEM(col_val.shape, BF16),
            pltpu.SMEM(near_row.shape, jnp.int32),
            pltpu.SMEM(owner_map.shape, jnp.int32),
            pltpu.SMEM(near_col.shape, jnp.int32),
            pltpu.VMEM((nz, points * tc, span), BF16),
            pltpu.VMEM((2, nx * 2 * tf, points * tc), BF16),
            pltpu.VMEM((2, nx * 3 * tf, points * tc), BF16),
            pltpu.VMEM((nc, groups, row_cond.shape[0] * cf, 128), BF16),
            pltpu.VMEM((nx, fine_rows, tf, tc), BF16),
            pltpu.VMEM((2, 128, tc), BF16),
            pltpu.VMEM((2, fine_rows * tf, fine_rows * cf), BF16),
            pltpu.VMEM((2 * row_cond.shape[0], tf, row_cond.shape[0] * cf), BF16),
            pltpu.VMEM((span, width), BF16),
            pltpu.VMEM((nx * nz * 2, tf, width), BF16),
            pltpu.VMEM((nz, nx - 1, 2, tf, width), BF16),
            pltpu.VMEM((nx * 6, tf, width), BF16),
            pltpu.SMEM((groups * fine_rows,), jnp.int32),
            pltpu.SMEM((groups * fine_rows,), jnp.int32),
            pltpu.SMEM((fine_rows,), jnp.int32),
            pltpu.SMEM((4, 2 * nx), jnp.int32),
            pltpu.SemaphoreType.DMA((2, nz // 2 + 1, points)),
            pltpu.SemaphoreType.DMA,
            pltpu.SemaphoreType.DMA((7,)),
            pltpu.SemaphoreType.DMA,
            pltpu.SemaphoreType.DMA((5,)),
            pltpu.SemaphoreType.DMA,
            pltpu.SemaphoreType.DMA((nx,)),
            pltpu.SemaphoreType.DMA,
            pltpu.SemaphoreType.DMA,
            pltpu.SemaphoreType.DMA,
        ],
        compiler_params=pltpu.CompilerParams(
            collective_id=0, has_side_effects=True, vmem_limit_bytes=60 * 1024 * 1024
        ),
    )(coarse, row_cond, row_val, col_cond, col_val, near_row, owner_map, near_col)


def solution(mesh, nz=Z_SIZE):
    nx, nc = mesh.shape["row"] // nz, mesh.shape["col"]
    return jax.shard_map(
        functools.partial(shards, nx, nz, nc),
        mesh=mesh,
        in_specs=(
            P("row", "col"),
            P(("row", "col"), None, None),
            P(("row", "col"), None, None),
            P("col", None, None),
            P("col", None, None),
            P(),
            P(),
            P("col"),
        ),
        out_specs=P("row", "col"),
        check_vma=False,
    )
```

```python
import functools

import jax
import jax.numpy as jnp
from jax import lax
from jax.experimental import pallas as pl
from jax.experimental.pallas import tpu as pltpu
from jax.sharding import PartitionSpec as P

MESH = pl.DeviceIdType.MESH
F32 = jnp.float32
BF16 = jnp.bfloat16
Z_SIZE = 16


def one_hot(shape, test):
    rows = lax.broadcasted_iota(jnp.int32, shape, 0)
    lanes = lax.broadcasted_iota(jnp.int32, shape, 1)
    return jnp.where(test(rows, lanes), 1.0, 0.0).astype(BF16)


def mm(a, b):
    return jnp.dot(a, b, preferred_element_type=F32)


def kernel(
    nx, nz, nc, cf, vf, cc, vc,
    coarse, row_cond_in, row_val_in, col_cond_in, col_val_in, near_row_in, owner_map_in, near_col_in,
    out,
    row_cond, row_val, col_cond, col_val, near_row, owner_map, near_col,
    kbuf, own_left, far_left, fbuf, pbuf, lane_pat, row_pat, pick, smat, ybuf, ysend, yfar,
    own_s, enc_s, sel_s, found,
    ready, ring_recv, ring_send, fetch_sem, local_sem, fac_recv, fac_send, x_recv, x_send, far_recv, far_send,
):
    me = lax.axis_index("row")
    my_col = lax.axis_index("col")
    my_x, my_z = me // nz, me % nz
    reach = nz // 2 - 2
    near = (-2, -1, 1, 2)
    groups = nx * (1 + len(near))
    tc, tf = cc * vc, cf * vf
    points = coarse.shape[0] // tc
    shift = points.bit_length() - 1
    assert points == 1 << shift
    fine_rows = out.shape[0] // tf
    width = out.shape[1]
    my_rows = row_cond.shape[0]
    row_shift = my_rows.bit_length() - 1
    assert my_rows == 1 << row_shift
    fac_rows = my_rows * cf

    z_up = (my_x * nz + (my_z + 1) % nz, my_col)
    z_down = (my_x * nz + (my_z + nz - 1) % nz, my_col)
    x_peer = [(((my_x + d) % nx) * nz + my_z, my_col) for d in range(nx)]
    col_peer = [(me, (my_col + d) % nc) for d in range(nc)]
    layer_peer = {
        dz: [(((my_x + d) % nx) * nz + (my_z + dz + nz) % nz, my_col) for d in range(nx)]
        for dz in near
    }

    barrier = pltpu.get_barrier_semaphore()

    def greet(semaphore, peer):
        pl.semaphore_signal(semaphore, inc=1, device_id=peer, device_id_type=MESH)

    def greet_peers(semaphore, higher):
        def x_one(x, carry):
            greet(semaphore, (x * nz + my_z, my_col))
            return carry

        def col_one(col, carry):
            greet(semaphore, (me, col))
            return carry

        if higher:
            lax.fori_loop(my_x + 1, nx, x_one, 0)
            lax.fori_loop(my_col + 1, nc, col_one, 0)
        else:
            lax.fori_loop(0, my_x, x_one, 0)
            lax.fori_loop(0, my_col, col_one, 0)
        for dz in near:
            z = (my_z + dz + nz) % nz
            planes = layer_peer[dz][1:] if abs(dz) == 1 else layer_peer[dz]

            @pl.when(z > my_z if higher else z < my_z)
            def _():
                for peer in planes:
                    greet(semaphore, peer)

    lower, count_all = my_x + my_col, nx - 1 + nc - 1
    for dz in near:
        planes = nx - 1 if abs(dz) == 1 else nx
        lower = lower + jnp.where((my_z + dz + nz) % nz < my_z, planes, 0)
        count_all += planes
    greet(barrier, z_up)
    greet(barrier, z_down)
    greet_peers(barrier, True)

    fetches = [
        pltpu.make_async_copy(source, target, fetch_sem.at[k])
        for k, (source, target) in enumerate((
            (row_cond_in, row_cond), (row_val_in, row_val), (near_row_in, near_row),
            (owner_map_in, owner_map), (near_col_in, near_col), (col_cond_in, col_cond),
            (col_val_in, col_val),
        ))
    ]
    for fetch in fetches:
        fetch.start()
    local = pltpu.make_async_copy(coarse, kbuf.at[my_z], local_sem)
    local.start()
    pl.semaphore_wait(barrier, 2 + lower)

    def ring_copy(way, hop, piece, src, first=False):
        rows = pl.ds(piece * tc, tc)
        source = coarse.at[rows, :] if first else kbuf.at[src, rows, :]
        return pltpu.make_async_remote_copy(
            src_ref=source,
            dst_ref=kbuf.at[src, rows, :],
            send_sem=ring_send,
            recv_sem=ring_recv.at[way, hop, piece],
            device_id=z_up if way == 0 else z_down,
            device_id_type=MESH,
        )

    def arrived(way, hop):
        return (my_z + nz - hop) % nz if way == 0 else (my_z + hop) % nz

    for piece in range(points):
        for way in (0, 1):
            ring_copy(way, 1, piece, my_z, first=True).start()

    for fetch in fetches[:2]:
        fetch.wait()
    greet_peers(ready, False)
    cond = row_cond[...].astype(F32).reshape(fac_rows, cc).astype(BF16)
    val = row_val[...].astype(F32)
    val = jnp.concatenate([val] * (cf // vf), axis=1).reshape(fac_rows, vc).astype(BF16)
    packed = mm(cond, one_hot((cc, 128), lambda k, l: l == k)) + mm(
        val, one_hot((vc, 128), lambda k, l: l == k + cc)
    )
    fbuf[my_col, my_x] = packed.astype(BF16)
    def move(src, dst, send, recv, peer):
        return pltpu.make_async_remote_copy(
            src_ref=src, dst_ref=dst, send_sem=send, recv_sem=recv, device_id=peer, device_id_type=MESH
        )

    def send_tiles():
        @pl.when(count_all > lower)
        def _():
            pl.semaphore_wait(ready, count_all - lower)

        mine = fbuf.at[my_col, my_x]
        for d in range(1, nx):
            move(mine, mine, fac_send, fac_recv.at[0], x_peer[d]).start()
        for dz in near:
            there = fbuf.at[my_col, nx + my_x * len(near) + near.index(-dz)]
            move(mine, there, fac_send, fac_recv.at[1], layer_peer[dz][0]).start()

    def group_place(g):
        far = (g - nx) % len(near)
        dz = far - 2 + jnp.where(far >= 2, 1, 0)
        x = jnp.where(g < nx, g, (g - nx) // len(near))
        return x, (my_z + jnp.where(g < nx, 0, dz) + nz) % nz

    def list_group(g):
        x, z = group_place(g)
        for i in range(fine_rows):
            slot = owner_map[near_row[(x * nz + z) * fine_rows + i]]
            own_s[g * fine_rows + i] = slot >> shift
            enc_s[g * fine_rows + i] = (i << shift) + (slot & (points - 1))

    def list_groups(start, count):
        def one(g, carry):
            list_group(g)
            return carry

        lax.fori_loop(start, start + count, one, 0)

    far_count = nx * len(near)
    layer_tiles = fbuf.at[my_col, pl.ds(0, nx)]
    near_tiles = fbuf.at[my_col, pl.ds(nx + my_x * len(near), len(near))]
    far_tiles = fbuf.at[my_col, pl.ds(nx, far_count)]

    def pass_layer_tiles():
        got = fbuf.at[my_col, pl.ds(0, nx - 1)]
        move(got, got, fac_send, fac_recv.at[0], x_peer[1]).wait_recv()
        for d in range(1, nc):
            move(layer_tiles, layer_tiles, fac_send, fac_recv.at[2], col_peer[d]).start()
        move(near_tiles, near_tiles, fac_send, fac_recv.at[1], z_up).wait_recv()
        for d in range(1, nx):
            move(near_tiles, near_tiles, fac_send, fac_recv.at[3], x_peer[d]).start()

    def pass_far_tiles():
        got = fbuf.at[my_col, pl.ds(nx, far_count - len(near))]
        move(got, got, fac_send, fac_recv.at[3], x_peer[1]).wait_recv()
        for d in range(1, nc):
            move(far_tiles, far_tiles, fac_send, fac_recv.at[4], col_peer[d]).start()

    def make_patterns():
        lane_pat[0] = one_hot((128, tc), lambda k, l: (k < cc) & (l // vc == k))
        lane_pat[1] = one_hot(
            (128, tc), lambda k, l: (k >= cc) & (k < cc + vc) & (l % vc == k - cc)
        )
        shape = row_pat.shape[1:]
        row_pat[0] = one_hot(shape, lambda t, k: t // vf == k)
        row_pat[1] = one_hot(shape, lambda t, k: (t // tf) * cf + t % vf == k)
        for row in range(my_rows):
            pick[row] = one_hot((tf, fac_rows), lambda t, k: k == row * cf + t // vf)
            pick[my_rows + row] = one_hot((tf, fac_rows), lambda t, k: k == row * cf + t % vf)

    def pairs(factors, entries):
        rows = entries * cf
        conds = mm(factors, lane_pat[0]).astype(BF16)
        vals = mm(factors, lane_pat[1]).astype(BF16)
        left = mm(row_pat[0, :entries * tf, :rows], conds)
        return left * mm(row_pat[1, :entries * tf, :rows], vals)

    def make_smat():
        fine_cols = col_cond.shape[0]
        ccond = col_cond[...].astype(F32).reshape(fine_cols * cf, cc).astype(BF16)
        cval = col_val[...].astype(F32)
        cval = jnp.concatenate([cval] * (cf // vf), axis=1)
        cval = cval.reshape(fine_cols * cf, vc).astype(BF16)
        cpacked = mm(ccond, one_hot((cc, 128), lambda k, l: l == k)) + mm(
            cval, one_hot((vc, 128), lambda k, l: l == k + cc)
        )
        right_pairs = pairs(cpacked.astype(BF16), fine_cols).T
        lane_point = jnp.zeros((1, width), jnp.int32)
        lane_f = lax.broadcasted_iota(jnp.int32, (1, width), 1) // tf
        for f in range(fine_cols):
            lane_point = jnp.where(lane_f == f, near_col[f], lane_point)
        for c in range(coarse.shape[1] // tc):
            smat[c * tc:(c + 1) * tc, :] = jnp.where(
                lane_point == c, right_pairs, 0.0
            ).astype(BF16)

    def make_sel():
        for i in range(fine_rows):
            o = own_s[my_x * fine_rows + i]
            second = jnp.int32(0)
            for k in range(i):
                second = jnp.where(own_s[my_x * fine_rows + k] == o, 1, second)
            sel_s[i] = o * 2 + second

    def find(z_src, k, group_of):
        o = my_x * nz + z_src
        for d in range(nx):
            base = group_of((my_x + d) % nx) * fine_rows
            first, last = jnp.int32(0), jnp.int32(0)
            hits = [(own_s[base + i] == o, enc_s[base + i]) for i in range(fine_rows)]
            for i in range(fine_rows):
                last = jnp.where(hits[i][0], hits[i][1], last)
                j = fine_rows - 1 - i
                first = jnp.where(hits[j][0], hits[j][1], first)
            found[k, 2 * d] = first
            found[k, 2 * d + 1] = last

    def own_group(x):
        return x

    def place_pair(left, way, at, entry, pair):
        point = entry & (points - 1)
        for p in range(points):
            left[way, at * tf:(at + 1) * tf, p * tc:(p + 1) * tc] = jnp.where(point == p, pair, 0)

    def prepare(z_src, way):
        find(z_src, way, own_group)
        for d in range(nx):
            for slot in range(2):
                entry = found[way, 2 * d + slot]
                pair = pbuf[(my_x + d) % nx, entry >> shift]
                place_pair(own_left, way, 2 * d + slot, entry, pair)

    def contract(left, z_src):
        partial = mm(left, kbuf[z_src]).astype(BF16)
        return mm(partial, smat[...]).astype(BF16).reshape(-1, tf, width)

    def finish(z_src, way):
        o = my_x * nz + z_src
        done = contract(own_left[way], z_src)
        for d in [*range(1, nx), 0]:
            rows = done[2 * d:2 * d + 2]
            if d == 0:
                ybuf[pl.ds(o * 2, 2)] = rows
                continue
            ysend[z_src, d - 1] = rows
            move(
                ysend.at[z_src, d - 1], ybuf.at[pl.ds(o * 2, 2)], x_send, x_recv.at[d], x_peer[d]
            ).start()

    def finish_far(z_src, way, sign):
        o = my_x * nz + z_src
        place = way * nx * 3
        yfar[place:place + nx * 3] = contract(far_left[way], z_src)
        for dz, slots, at in ((2 * sign, (way,), place), (sign, (0, 1), place + nx)):
            for d in range(nx):
                move(
                    yfar.at[pl.ds(at + d * len(slots), len(slots))],
                    ybuf.at[pl.ds(o * 2 + slots[0], len(slots))],
                    far_send, far_recv, layer_peer[dz][d],
                ).start()

    def prepare_far(way, sign):
        left, right, entries = [], [], []
        z_src = arrived(way, reach)
        for k, dz, slots in ((2, 2 * sign, (way,)), (3, sign, (0, 1))):
            find(z_src, k, lambda x: nx + x * len(near) + near.index(dz))
            for d in range(nx):
                group = nx + ((my_x + d) % nx) * len(near) + near.index(dz)
                for slot in slots:
                    entry = found[k, 2 * d + slot]
                    row = entry >> shift
                    tile = fbuf[row >> row_shift, group]
                    row = row & (my_rows - 1)
                    entries.append(entry)
                    left.append(mm(pick[row], tile).astype(BF16))
                    right.append(mm(pick[my_rows + row], tile).astype(BF16))
        product = mm(jnp.concatenate(left, axis=0), lane_pat[0]) * mm(
            jnp.concatenate(right, axis=0), lane_pat[1]
        )
        product = product.astype(BF16)
        for at, entry in enumerate(entries):
            place_pair(far_left, way, at, entry, product[at * tf:(at + 1) * tf])

    def forward(hop, piece):
        for way in (0, 1):
            z_src = arrived(way, hop - 1)
            ring_copy(way, hop - 1, piece, z_src).wait_recv()
            ring_copy(way, hop, piece, z_src).start()

    def first_lists():
        for fetch in fetches[2:]:
            fetch.wait()
        list_groups(0, nx)
        make_sel()

    def make_pairs():
        got = fbuf.at[pl.ds(0, nc - 1), pl.ds(0, nx)]
        move(got, got, fac_send, fac_recv.at[2], col_peer[1]).wait_recv()
        for g in range(nx):
            factors = fbuf[:, g].reshape(nc * fac_rows, 128)
            pbuf[g] = pairs(factors, fine_rows).astype(BF16).reshape(fine_rows, tf, tc)

    def finish_chunk(hop, way):
        def task():
            z_src = arrived(way, hop)
            prepare(z_src, way)
            finish(z_src, way)

        return task

    share = far_count // 4

    def near_lists(k):
        return lambda: list_groups(nx + k * share, share)

    tasks = [first_lists, send_tiles, make_patterns, make_smat]
    tasks += [pass_layer_tiles, near_lists(0), pass_far_tiles, make_pairs]
    chunks = [finish_chunk(hop, way) for hop in range(1, reach) for way in (0, 1)]
    tasks += [finish_chunk(0, 0)] + chunks[:6] + [near_lists(1)] + chunks[6:8]
    tasks += [near_lists(2), near_lists(3)] + chunks[8:]
    local.wait()
    for hop in range(2, reach + 1):
        for piece in range(points):
            forward(hop, piece)
            tasks.pop(0)()
    for task in tasks:
        task()
    got = fbuf.at[pl.ds(0, nc - 1), pl.ds(nx, far_count)]
    move(got, got, fac_send, fac_recv.at[4], col_peer[1]).wait_recv()
    sides = ((0, 1), (1, -1))
    for way, sign in sides:
        prepare_far(way, sign)
        prepare(arrived(way, reach), way)
    for way, sign in sides:
        z_src = arrived(way, reach)
        for piece in range(points):
            ring_copy(way, reach, piece, z_src).wait_recv()
        finish_far(z_src, way, sign)
        finish(z_src, way)

    for d in range(1, nx):
        block = ybuf.at[pl.ds(0, (2 * reach + 1) * 2)]
        move(block, block, x_send, x_recv.at[d], x_peer[d]).wait_recv()
    block = ybuf.at[pl.ds(0, nx * 6)]
    move(block, block, far_send, far_recv, x_peer[1]).wait_recv()
    for i in range(fine_rows):
        out[i * tf:(i + 1) * tf, :] = ybuf[sel_s[i]]

    move(block, block, far_send, far_recv, x_peer[1]).wait_send()
    ring = kbuf.at[pl.ds(0, 2 * reach)]
    move(ring, ring, ring_send, ring_recv.at[0, 0, 0], z_up).wait_send()
    block = ysend.at[pl.ds(0, 2 * reach + 1)]
    move(block, block, x_send, x_recv.at[0], x_peer[1]).wait_send()
    for sent in (
        fbuf.at[0, pl.ds(0, nx - 1)], fbuf.at[0, pl.ds(0, len(near))],
        fbuf.at[pl.ds(0, nc - 1), pl.ds(0, nx)], fbuf.at[pl.ds(0, nx - 1), pl.ds(0, len(near))],
        fbuf.at[pl.ds(0, nc - 1), pl.ds(nx, far_count)],
    ):
        move(sent, sent, fac_send, fac_recv.at[0], x_peer[1]).wait_send()


def shards(nx, nz, nc, coarse, row_cond, row_val, col_cond, col_val, near_row, owner_map, near_col):
    cf, cc = row_cond.shape[1:]
    vf, vc = row_val.shape[1:]
    tc, tf = cc * vc, cf * vf
    points = coarse.shape[0] // tc
    fine_rows = row_cond.shape[0] * nc
    width = col_cond.shape[0] * tf
    groups = nx * 5
    span = coarse.shape[1]
    return pl.pallas_call(
        functools.partial(kernel, nx, nz, nc, cf, vf, cc, vc),
        out_shape=pltpu.VMEM((fine_rows * tf, width), BF16),
        in_specs=[pl.BlockSpec(memory_space=pltpu.HBM)] * 8,
        out_specs=pl.BlockSpec(memory_space=pltpu.VMEM),
        scratch_shapes=[
            pltpu.VMEM(row_cond.shape, BF16),
            pltpu.VMEM(row_val.shape, BF16),
            pltpu.VMEM(col_cond.shape, BF16),
            pltpu.VMEM(col_val.shape, BF16),
            pltpu.SMEM(near_row.shape, jnp.int32),
            pltpu.SMEM(owner_map.shape, jnp.int32),
            pltpu.SMEM(near_col.shape, jnp.int32),
            pltpu.VMEM((nz, points * tc, span), BF16),
            pltpu.VMEM((2, nx * 2 * tf, points * tc), BF16),
            pltpu.VMEM((2, nx * 3 * tf, points * tc), BF16),
            pltpu.VMEM((nc, groups, row_cond.shape[0] * cf, 128), BF16),
            pltpu.VMEM((nx, fine_rows, tf, tc), BF16),
            pltpu.VMEM((2, 128, tc), BF16),
            pltpu.VMEM((2, fine_rows * tf, fine_rows * cf), BF16),
            pltpu.VMEM((2 * row_cond.shape[0], tf, row_cond.shape[0] * cf), BF16),
            pltpu.VMEM((span, width), BF16),
            pltpu.VMEM((nx * nz * 2, tf, width), BF16),
            pltpu.VMEM((nz, nx - 1, 2, tf, width), BF16),
            pltpu.VMEM((nx * 6, tf, width), BF16),
            pltpu.SMEM((groups * fine_rows,), jnp.int32),
            pltpu.SMEM((groups * fine_rows,), jnp.int32),
            pltpu.SMEM((fine_rows,), jnp.int32),
            pltpu.SMEM((4, 2 * nx), jnp.int32),
            pltpu.SemaphoreType.REGULAR,
            pltpu.SemaphoreType.DMA((2, nz // 2 + 1, points)),
            pltpu.SemaphoreType.DMA,
            pltpu.SemaphoreType.DMA((7,)),
            pltpu.SemaphoreType.DMA,
            pltpu.SemaphoreType.DMA((5,)),
            pltpu.SemaphoreType.DMA,
            pltpu.SemaphoreType.DMA((nx,)),
            pltpu.SemaphoreType.DMA,
            pltpu.SemaphoreType.DMA,
            pltpu.SemaphoreType.DMA,
        ],
        compiler_params=pltpu.CompilerParams(
            collective_id=0, has_side_effects=True, vmem_limit_bytes=60 * 1024 * 1024
        ),
    )(coarse, row_cond, row_val, col_cond, col_val, near_row, owner_map, near_col)


def solution(mesh, nz=Z_SIZE):
    nx, nc = mesh.shape["row"] // nz, mesh.shape["col"]
    return jax.shard_map(
        functools.partial(shards, nx, nz, nc),
        mesh=mesh,
        in_specs=(
            P("row", "col"),
            P(("row", "col"), None, None),
            P(("row", "col"), None, None),
            P("col", None, None),
            P("col", None, None),
            P(),
            P(),
            P("col"),
        ),
        out_specs=P("row", "col"),
        check_vma=False,
    )
```

```python
import functools

import jax
import jax.numpy as jnp
from jax import lax
from jax.experimental import pallas as pl
from jax.experimental.pallas import tpu as pltpu
from jax.sharding import PartitionSpec as P

MESH = pl.DeviceIdType.MESH
F32 = jnp.float32
BF16 = jnp.bfloat16
Z_SIZE = 16


def one_hot(shape, test):
    rows = lax.broadcasted_iota(jnp.int32, shape, 0)
    lanes = lax.broadcasted_iota(jnp.int32, shape, 1)
    return jnp.where(test(rows, lanes), 1.0, 0.0).astype(BF16)


def mm(a, b):
    return jnp.dot(a, b, preferred_element_type=F32)


def kernel(
    nx, nz, nc, cf, vf, cc, vc,
    coarse, row_cond_in, row_val_in, col_cond_in, col_val_in, near_row_in, owner_map_in, near_col_in,
    out,
    row_cond, row_val, col_cond, col_val, near_row, owner_map, near_col,
    kbuf, own_left, far_left, fbuf, pbuf, lane_pat, row_pat, pick, smat, ybuf, ysend, yfar, ysel,
    own_s, enc_s, sel_s, found,
    ready, ring_recv, ring_send, fetch_sem, local_sem, fac_recv, fac_send, x_recv, x_send, far_recv, far_send,
):
    me = lax.axis_index("row")
    my_col = lax.axis_index("col")
    my_x, my_z = me // nz, me % nz
    reach = nz // 2 - 2
    near = (-2, -1, 1, 2)
    groups = nx * (1 + len(near))
    tc, tf = cc * vc, cf * vf
    points = coarse.shape[0] // tc
    shift = points.bit_length() - 1
    assert points == 1 << shift
    fine_rows = out.shape[0] // tf
    width = out.shape[1]
    my_rows = row_cond.shape[0]
    row_shift = my_rows.bit_length() - 1
    assert my_rows == 1 << row_shift
    fac_rows = my_rows * cf
    lanes, block_rows = coarse.shape[1] // 2, coarse.shape[0] // 2

    z_up = (my_x * nz + (my_z + 1) % nz, my_col)
    z_down = (my_x * nz + (my_z + nz - 1) % nz, my_col)
    x_peer = [(((my_x + d) % nx) * nz + my_z, my_col) for d in range(nx)]
    col_peer = [(me, (my_col + d) % nc) for d in range(nc)]
    layer_peer = {
        dz: [(((my_x + d) % nx) * nz + (my_z + dz + nz) % nz, my_col) for d in range(nx)]
        for dz in near
    }

    barrier = pltpu.get_barrier_semaphore()

    def greet(semaphore, peer):
        pl.semaphore_signal(semaphore, inc=1, device_id=peer, device_id_type=MESH)

    def greet_peers(semaphore, higher):
        def x_one(x, carry):
            greet(semaphore, (x * nz + my_z, my_col))
            return carry

        def col_one(col, carry):
            greet(semaphore, (me, col))
            return carry

        if higher:
            lax.fori_loop(my_x + 1, nx, x_one, 0)
            lax.fori_loop(my_col + 1, nc, col_one, 0)
        else:
            lax.fori_loop(0, my_x, x_one, 0)
            lax.fori_loop(0, my_col, col_one, 0)
        for dz in near:
            z = (my_z + dz + nz) % nz
            planes = layer_peer[dz][1:] if abs(dz) == 1 else layer_peer[dz]

            @pl.when(z > my_z if higher else z < my_z)
            def _():
                for peer in planes:
                    greet(semaphore, peer)

    lower, count_all = my_x + my_col, nx - 1 + nc - 1
    for dz in near:
        planes = nx - 1 if abs(dz) == 1 else nx
        lower = lower + jnp.where((my_z + dz + nz) % nz < my_z, planes, 0)
        count_all += planes
    greet(barrier, z_up)
    greet(barrier, z_down)
    greet_peers(barrier, True)

    fetches = [
        pltpu.make_async_copy(source, target, fetch_sem.at[k])
        for k, (source, target) in enumerate((
            (row_cond_in, row_cond), (row_val_in, row_val), (near_row_in, near_row),
            (owner_map_in, owner_map), (near_col_in, near_col), (col_cond_in, col_cond),
            (col_val_in, col_val),
        ))
    ]
    for fetch in fetches:
        fetch.start()
    locals_ = [
        pltpu.make_async_copy(
            coarse.at[:, pl.ds(part * lanes, lanes)], kbuf.at[my_z, part], local_sem.at[part]
        )
        for part in (0, 1)
    ]
    for local in locals_:
        local.start()
    pl.semaphore_wait(barrier, 2 + lower)

    def ring_copy(way, hop, piece, src, first=False):
        part, rows = piece // 2, pl.ds((piece % 2) * block_rows, block_rows)
        target = kbuf.at[src, part, rows, :]
        source = coarse.at[rows, pl.ds(part * lanes, lanes)] if first else target
        return pltpu.make_async_remote_copy(
            src_ref=source,
            dst_ref=target,
            send_sem=ring_send,
            recv_sem=ring_recv.at[way, hop, piece],
            device_id=z_up if way == 0 else z_down,
            device_id_type=MESH,
        )

    def arrived(way, hop):
        return (my_z + nz - hop) % nz if way == 0 else (my_z + hop) % nz

    for piece in range(points):
        for way in (0, 1):
            ring_copy(way, 1, piece, my_z, first=True).start()

    for fetch in fetches[:2]:
        fetch.wait()
    greet_peers(ready, False)
    cond = row_cond[...].astype(F32).reshape(fac_rows, cc).astype(BF16)
    val = row_val[...].astype(F32)
    val = jnp.concatenate([val] * (cf // vf), axis=1).reshape(fac_rows, vc).astype(BF16)
    packed = mm(cond, one_hot((cc, 128), lambda k, l: l == k)) + mm(
        val, one_hot((vc, 128), lambda k, l: l == k + cc)
    )
    fbuf[my_col, my_x] = packed.astype(BF16)
    def move(src, dst, send, recv, peer):
        return pltpu.make_async_remote_copy(
            src_ref=src, dst_ref=dst, send_sem=send, recv_sem=recv, device_id=peer, device_id_type=MESH
        )

    def send_tiles():
        @pl.when(count_all > lower)
        def _():
            pl.semaphore_wait(ready, count_all - lower)

        mine = fbuf.at[my_col, my_x]
        for d in range(1, nx):
            move(mine, mine, fac_send, fac_recv.at[0], x_peer[d]).start()
        for dz in near:
            there = fbuf.at[my_col, nx + my_x * len(near) + near.index(-dz)]
            move(mine, there, fac_send, fac_recv.at[1], layer_peer[dz][0]).start()

    def group_place(g):
        far = (g - nx) % len(near)
        dz = far - 2 + jnp.where(far >= 2, 1, 0)
        x = jnp.where(g < nx, g, (g - nx) // len(near))
        return x, (my_z + jnp.where(g < nx, 0, dz) + nz) % nz

    def list_group(g):
        x, z = group_place(g)
        for i in range(fine_rows):
            slot = owner_map[near_row[(x * nz + z) * fine_rows + i]]
            own_s[g * fine_rows + i] = slot >> shift
            enc_s[g * fine_rows + i] = (i << shift) + (slot & (points - 1))

    def list_groups(start, count):
        def one(g, carry):
            list_group(g)
            return carry

        lax.fori_loop(start, start + count, one, 0)

    far_count = nx * len(near)
    layer_tiles = fbuf.at[my_col, pl.ds(0, nx)]
    near_tiles = fbuf.at[my_col, pl.ds(nx + my_x * len(near), len(near))]
    far_tiles = fbuf.at[my_col, pl.ds(nx, far_count)]

    def pass_layer_tiles():
        got = fbuf.at[my_col, pl.ds(0, nx - 1)]
        move(got, got, fac_send, fac_recv.at[0], x_peer[1]).wait_recv()
        for d in range(1, nc):
            move(layer_tiles, layer_tiles, fac_send, fac_recv.at[2], col_peer[d]).start()
        move(near_tiles, near_tiles, fac_send, fac_recv.at[1], z_up).wait_recv()
        for d in range(1, nx):
            move(near_tiles, near_tiles, fac_send, fac_recv.at[3], x_peer[d]).start()

    def pass_far_tiles():
        got = fbuf.at[my_col, pl.ds(nx, far_count - len(near))]
        move(got, got, fac_send, fac_recv.at[3], x_peer[1]).wait_recv()
        for d in range(1, nc):
            move(far_tiles, far_tiles, fac_send, fac_recv.at[4], col_peer[d]).start()

    def make_patterns():
        lane_pat[0] = one_hot((128, tc), lambda k, l: (k < cc) & (l // vc == k))
        lane_pat[1] = one_hot(
            (128, tc), lambda k, l: (k >= cc) & (k < cc + vc) & (l % vc == k - cc)
        )
        shape = row_pat.shape[1:]
        row_pat[0] = one_hot(shape, lambda t, k: t // vf == k)
        row_pat[1] = one_hot(shape, lambda t, k: (t // tf) * cf + t % vf == k)
        for row in range(my_rows):
            pick[row] = one_hot((tf, fac_rows), lambda t, k: k == row * cf + t // vf)
            pick[my_rows + row] = one_hot((tf, fac_rows), lambda t, k: k == row * cf + t % vf)

    def pairs(factors, entries):
        rows = entries * cf
        conds = mm(factors, lane_pat[0]).astype(BF16)
        vals = mm(factors, lane_pat[1]).astype(BF16)
        left = mm(row_pat[0, :entries * tf, :rows], conds)
        return left * mm(row_pat[1, :entries * tf, :rows], vals)

    def make_smat():
        fine_cols = col_cond.shape[0]
        ccond = col_cond[...].astype(F32).reshape(fine_cols * cf, cc).astype(BF16)
        cval = col_val[...].astype(F32)
        cval = jnp.concatenate([cval] * (cf // vf), axis=1)
        cval = cval.reshape(fine_cols * cf, vc).astype(BF16)
        cpacked = mm(ccond, one_hot((cc, 128), lambda k, l: l == k)) + mm(
            cval, one_hot((vc, 128), lambda k, l: l == k + cc)
        )
        right_pairs = pairs(cpacked.astype(BF16), fine_cols).T
        lane_point = jnp.zeros((1, width), jnp.int32)
        lane_f = lax.broadcasted_iota(jnp.int32, (1, width), 1) // tf
        for f in range(fine_cols):
            lane_point = jnp.where(lane_f == f, near_col[f], lane_point)
        for c in range(coarse.shape[1] // tc):
            smat[c * tc:(c + 1) * tc, :] = jnp.where(
                lane_point == c, right_pairs, 0.0
            ).astype(BF16)

    def make_sel():
        for i in range(fine_rows):
            o = own_s[my_x * fine_rows + i]
            second = jnp.int32(0)
            for k in range(i):
                second = jnp.where(own_s[my_x * fine_rows + k] == o, 1, second)
            sel_s[i] = o * 2 + second

    def find(z_src, k, group_of):
        o = my_x * nz + z_src
        for d in range(nx):
            base = group_of((my_x + d) % nx) * fine_rows
            first, last = jnp.int32(0), jnp.int32(0)
            hits = [(own_s[base + i] == o, enc_s[base + i]) for i in range(fine_rows)]
            for i in range(fine_rows):
                last = jnp.where(hits[i][0], hits[i][1], last)
                j = fine_rows - 1 - i
                first = jnp.where(hits[j][0], hits[j][1], first)
            found[k, 2 * d] = first
            found[k, 2 * d + 1] = last

    def own_group(x):
        return x

    def place_pair(left, way, at, entry, pair):
        point = entry & (points - 1)
        for p in range(points):
            left[way, at * tf:(at + 1) * tf, p * tc:(p + 1) * tc] = jnp.where(point == p, pair, 0)

    def prepare(z_src, way):
        find(z_src, way, own_group)
        for d in range(nx):
            for slot in range(2):
                entry = found[way, 2 * d + slot]
                pair = pbuf[(my_x + d) % nx, entry >> shift]
                place_pair(own_left, way, 2 * d + slot, entry, pair)

    def contract(left, z_src, part):
        return mm(left, kbuf[z_src, part]).astype(BF16).reshape(-1, tf, lanes)

    def finish(z_src, way, parts=(0, 1)):
        o = my_x * nz + z_src
        done = [contract(own_left[way], z_src, part) for part in parts]
        for d in [*range(1, nx), 0]:
            for part, rows in zip(parts, done):
                if d == 0:
                    ybuf[part, pl.ds(o * 2, 2)] = rows[:2]
                else:
                    ysend[z_src, d - 1, part] = rows[2 * d:2 * d + 2]
            if d == 0:
                continue
            span = pl.ds(parts[0], len(parts))
            move(
                ysend.at[z_src, d - 1, span], ybuf.at[span, pl.ds(o * 2, 2)],
                x_send, x_recv.at[d], x_peer[d],
            ).start()

    def finish_far(z_src, way, sign, part):
        o = my_x * nz + z_src
        place = way * nx * 3
        yfar[part, place:place + nx * 3] = contract(far_left[way], z_src, part)
        for dz, slots, at in ((2 * sign, (way,), place), (sign, (0, 1), place + nx)):
            for d in range(nx):
                move(
                    yfar.at[part, pl.ds(at + d * len(slots), len(slots))],
                    ybuf.at[part, pl.ds(o * 2 + slots[0], len(slots))],
                    far_send, far_recv, layer_peer[dz][d],
                ).start()

    def prepare_far(way, sign):
        left, right, entries = [], [], []
        z_src = arrived(way, reach)
        for k, dz, slots in ((2, 2 * sign, (way,)), (3, sign, (0, 1))):
            find(z_src, k, lambda x: nx + x * len(near) + near.index(dz))
            for d in range(nx):
                group = nx + ((my_x + d) % nx) * len(near) + near.index(dz)
                for slot in slots:
                    entry = found[k, 2 * d + slot]
                    row = entry >> shift
                    tile = fbuf[row >> row_shift, group]
                    row = row & (my_rows - 1)
                    entries.append(entry)
                    left.append(mm(pick[row], tile).astype(BF16))
                    right.append(mm(pick[my_rows + row], tile).astype(BF16))
        product = mm(jnp.concatenate(left, axis=0), lane_pat[0]) * mm(
            jnp.concatenate(right, axis=0), lane_pat[1]
        )
        product = product.astype(BF16)
        for at, entry in enumerate(entries):
            place_pair(far_left, way, at, entry, product[at * tf:(at + 1) * tf])

    def forward(hop, piece):
        for way in (0, 1):
            z_src = arrived(way, hop - 1)
            ring_copy(way, hop - 1, piece, z_src).wait_recv()
            ring_copy(way, hop, piece, z_src).start()

    def first_lists():
        for fetch in fetches[2:]:
            fetch.wait()
        list_groups(0, nx)
        make_sel()

    def make_pairs():
        got = fbuf.at[pl.ds(0, nc - 1), pl.ds(0, nx)]
        move(got, got, fac_send, fac_recv.at[2], col_peer[1]).wait_recv()
        for g in range(nx):
            factors = fbuf[:, g].reshape(nc * fac_rows, 128)
            pbuf[g] = pairs(factors, fine_rows).astype(BF16).reshape(fine_rows, tf, tc)

    def finish_chunk(hop, way):
        def task():
            z_src = arrived(way, hop)
            prepare(z_src, way)
            finish(z_src, way)

        return task

    share = far_count // 4

    def near_lists(k):
        return lambda: list_groups(nx + k * share, share)

    def pass_far_and_list():
        pass_far_tiles()
        list_groups(nx + share, share)

    def prepare_both(hop):
        for way in (0, 1):
            prepare(arrived(way, hop), way)

    def list_last():
        list_groups(nx + 3 * share, share)
        prepare_both(reach - 1)

    chunks = [finish_chunk(hop, way) for hop in range(1, reach - 1) for way in (0, 1)]
    tasks = [first_lists, send_tiles, make_patterns, make_smat]
    tasks += [pass_layer_tiles, near_lists(0), pass_far_and_list, make_pairs]
    tasks += [finish_chunk(0, 0)] + chunks[:6] + [near_lists(2)] + chunks[6:] + [list_last]
    for local in locals_:
        local.wait()
    for hop in range(2, reach + 1):
        for piece in range(points):
            forward(hop, piece)
            if tasks:
                tasks.pop(0)()
    for way in (0, 1):
        finish(arrived(way, reach - 1), way)
    got = fbuf.at[pl.ds(0, nc - 1), pl.ds(nx, far_count)]
    move(got, got, fac_send, fac_recv.at[4], col_peer[1]).wait_recv()
    sides = ((0, 1), (1, -1))
    for way, sign in sides:
        prepare_far(way, sign)
        prepare(arrived(way, reach), way)
    for part in (0, 1):
        for way, sign in sides:
            z_src = arrived(way, reach)
            for piece in (2 * part, 2 * part + 1):
                ring_copy(way, reach, piece, z_src).wait_recv()
            finish_far(z_src, way, sign, part)
            finish(z_src, way, (part,))

    for d in range(1, nx):
        block = ybuf.at[:, pl.ds(0, (2 * reach + 1) * 2)]
        move(block, block, x_send, x_recv.at[d], x_peer[d]).wait_recv()
    block = ybuf.at[:, pl.ds(0, nx * 6)]
    move(block, block, far_send, far_recv, x_peer[1]).wait_recv()
    for i in range(fine_rows):
        for part in (0, 1):
            ysel[i * tf:(i + 1) * tf, part * lanes:(part + 1) * lanes] = ybuf[part, sel_s[i]]
    out[...] = mm(ysel[...], smat[...]).astype(BF16)

    move(block, block, far_send, far_recv, x_peer[1]).wait_send()
    ring = kbuf.at[pl.ds(0, 2 * reach)]
    move(ring, ring, ring_send, ring_recv.at[0, 0, 0], z_up).wait_send()
    block = ysend.at[pl.ds(0, 2 * reach + 1)]
    move(block, block, x_send, x_recv.at[0], x_peer[1]).wait_send()
    for sent in (
        fbuf.at[0, pl.ds(0, nx - 1)], fbuf.at[0, pl.ds(0, len(near))],
        fbuf.at[pl.ds(0, nc - 1), pl.ds(0, nx)], fbuf.at[pl.ds(0, nx - 1), pl.ds(0, len(near))],
        fbuf.at[pl.ds(0, nc - 1), pl.ds(nx, far_count)],
    ):
        move(sent, sent, fac_send, fac_recv.at[0], x_peer[1]).wait_send()


def shards(nx, nz, nc, coarse, row_cond, row_val, col_cond, col_val, near_row, owner_map, near_col):
    cf, cc = row_cond.shape[1:]
    vf, vc = row_val.shape[1:]
    tc, tf = cc * vc, cf * vf
    points = coarse.shape[0] // tc
    fine_rows = row_cond.shape[0] * nc
    width = col_cond.shape[0] * tf
    groups = nx * 5
    span = coarse.shape[1]
    return pl.pallas_call(
        functools.partial(kernel, nx, nz, nc, cf, vf, cc, vc),
        out_shape=pltpu.VMEM((fine_rows * tf, width), BF16),
        in_specs=[pl.BlockSpec(memory_space=pltpu.HBM)] * 8,
        out_specs=pl.BlockSpec(memory_space=pltpu.VMEM),
        scratch_shapes=[
            pltpu.VMEM(row_cond.shape, BF16),
            pltpu.VMEM(row_val.shape, BF16),
            pltpu.VMEM(col_cond.shape, BF16),
            pltpu.VMEM(col_val.shape, BF16),
            pltpu.SMEM(near_row.shape, jnp.int32),
            pltpu.SMEM(owner_map.shape, jnp.int32),
            pltpu.SMEM(near_col.shape, jnp.int32),
            pltpu.VMEM((nz, 2, points * tc, span // 2), BF16),
            pltpu.VMEM((2, nx * 2 * tf, points * tc), BF16),
            pltpu.VMEM((2, nx * 3 * tf, points * tc), BF16),
            pltpu.VMEM((nc, groups, row_cond.shape[0] * cf, 128), BF16),
            pltpu.VMEM((nx, fine_rows, tf, tc), BF16),
            pltpu.VMEM((2, 128, tc), BF16),
            pltpu.VMEM((2, fine_rows * tf, fine_rows * cf), BF16),
            pltpu.VMEM((2 * row_cond.shape[0], tf, row_cond.shape[0] * cf), BF16),
            pltpu.VMEM((span, width), BF16),
            pltpu.VMEM((2, nx * nz * 2, tf, span // 2), BF16),
            pltpu.VMEM((nz, nx - 1, 2, 2, tf, span // 2), BF16),
            pltpu.VMEM((2, nx * 6, tf, span // 2), BF16),
            pltpu.VMEM((fine_rows * tf, span), BF16),
            pltpu.SMEM((groups * fine_rows,), jnp.int32),
            pltpu.SMEM((groups * fine_rows,), jnp.int32),
            pltpu.SMEM((fine_rows,), jnp.int32),
            pltpu.SMEM((4, 2 * nx), jnp.int32),
            pltpu.SemaphoreType.REGULAR,
            pltpu.SemaphoreType.DMA((2, nz // 2 + 1, points)),
            pltpu.SemaphoreType.DMA,
            pltpu.SemaphoreType.DMA((7,)),
            pltpu.SemaphoreType.DMA((2,)),
            pltpu.SemaphoreType.DMA((5,)),
            pltpu.SemaphoreType.DMA,
            pltpu.SemaphoreType.DMA((nx,)),
            pltpu.SemaphoreType.DMA,
            pltpu.SemaphoreType.DMA,
            pltpu.SemaphoreType.DMA,
        ],
        compiler_params=pltpu.CompilerParams(
            collective_id=0, has_side_effects=True, vmem_limit_bytes=60 * 1024 * 1024
        ),
    )(coarse, row_cond, row_val, col_cond, col_val, near_row, owner_map, near_col)


def solution(mesh, nz=Z_SIZE):
    nx, nc = mesh.shape["row"] // nz, mesh.shape["col"]
    return jax.shard_map(
        functools.partial(shards, nx, nz, nc),
        mesh=mesh,
        in_specs=(
            P("row", "col"),
            P(("row", "col"), None, None),
            P(("row", "col"), None, None),
            P("col", None, None),
            P("col", None, None),
            P(),
            P(),
            P("col"),
        ),
        out_specs=P("row", "col"),
        check_vma=False,
    )
```
